32 devices in a mesh: dp: 4 (over x, core), section: 2 (over y), tensor: 4 (over z).
Axes of the slice: x: 2, y: 2, z: 4, core: 2. Of those that a mesh axis runs over, the one named last changes fastest.
Arguments:
- arrivals: bfloat16 [2, 4, 128, 4096], P('section', 'dp', None, 'tensor'), may hold values from -30 to 30
- fresh: bfloat16 [2, 4, 128, 4096], P(None, 'dp', None, 'tensor'), may hold values from -30 to 30
- stash: bfloat16 [2, 2, 4, 128, 4096], P(None, 'section', 'dp', None, 'tensor'), may hold values from -30 to 30
- returning: bfloat16 [2, 4, 128, 4096], P('section', 'dp', None, 'tensor'), may hold values from -6 to 6
- loss_grad: bfloat16 [2, 4, 128, 4096], P(None, 'dp', None, 'tensor'), may hold values from -6 to 6
- gain: float32 [2, 4096], P('section', 'tensor'), may hold values from 0.1 to 1.9
- query_weight: bfloat16 [2, 4096, 4096], P('section', 'dp', 'tensor'), may hold values from -0.09375 to 0.09375
- key_weight: bfloat16 [2, 4096, 1024], P('section', 'dp', 'tensor'), may hold values from -0.09375 to 0.09375
- value_weight: bfloat16 [2, 4096, 1024], P('section', 'dp', 'tensor'), may hold values from -0.09375 to 0.09375
- w_out: bfloat16 [2, 4096, 4096], P('section', 'dp', 'tensor'), may hold values from -0.09375 to 0.09375
- plan: int32 [2, 4], replicated, may hold values from 0 to 3, each once within a row
- fresh_docs: int32 [2, 4, 128], replicated, may hold values from 0 to 5, never falling along the last dimension, each value on 1 to 64 neighbouring positions
- arrival_docs: int32 [2, 4, 128], P(None, 'dp'), may hold values from 0 to 5, never falling along the last dimension, each value on 1 to 64 neighbouring positions
- stash_docs: int32 [2, 2, 4, 128], P(None, 'section', 'dp'), may hold values from 0 to 5, never falling along the last dimension, each value on 1 to 64 neighbouring positions
Outputs:
- sent_forward: bfloat16 [2, 4, 128, 4096], P('section', 'dp', None, 'tensor')
- sent_backward: bfloat16 [2, 4, 128, 4096], P('section', 'dp', None, 'tensor')
- gain_grad: float32 [2, 4096], P('section', 'tensor')
The draws below stay inside these ranges and needn't reach their ends.
Inputs may be any that keep to these rules, and one draw needn't show every extreme that they name: Each row of plan names every packed row of its micro-batch once. `fresh_docs`: along a packed row document numbers never fall; every document holds 1 to 64 tokens and one holds exactly 64. `arrival_docs`: along a packed row document numbers never fall; every document holds 1 to 64 tokens and one holds exactly 64. `stash_docs`: along a packed row document numbers never fall; every document holds 1 to 64 tokens and one holds exactly 64.
All inputs are finite; a program needn't handle non-finite values.
Results may differ from the reference program's by a relative error of at most 0.035.
Values may be sent and summed in bfloat16 or wider, within the bound.
No kernel may reach another device: no remote copies, remote signals or barrier semaphores. Data moves between devices by JAX's collectives and lax.ppermute only.
A program may use at most 64 MiB of HBM per device.

```python
import math
import jax
import jax.numpy as jnp
import numpy as np
from jax import lax

MODEL_WIDTH = 4096
QUERY_HEADS = 32
KEY_VALUE_HEADS = 8
HEAD_SIZE = 128
ROW_TOKENS = 128
TICKS = 2
DOCS = 6
DOC_MOST = 64
SECTION_LAYERS = 2
PACKS = 4
N_TENSOR = 4


def activation_rows(key, shape):
    key_base, key_row = jax.random.split(jax.random.fold_in(key, 11))
    column = jnp.arange(shape[-1], dtype=jnp.float32) / shape[-1]
    row_scale = 10.0 ** jax.random.uniform(key_row, shape[:-1] + (1,), minval=0.0, maxval=0.3)
    base = jnp.clip(jax.random.normal(key_base, shape), -5.0, 5.0)
    column_scale = 10.0 ** column
    values = 0.3 * base * row_scale * column_scale
    return values.astype(jnp.float32).astype(jnp.bfloat16)


def draw_arrivals(key, part):
    return activation_rows(jax.random.fold_in(key, 1), (SECTION_LAYERS, PACKS, ROW_TOKENS, MODEL_WIDTH))


def draw_fresh(key, part):
    return activation_rows(jax.random.fold_in(key, 2), (TICKS, PACKS, ROW_TOKENS, MODEL_WIDTH))


def draw_stash(key, part):
    return activation_rows(jax.random.fold_in(key, 3), (TICKS, SECTION_LAYERS, PACKS, ROW_TOKENS, MODEL_WIDTH))


def block_levels(rng, dims, shards, least, largest):
    factor_of = 1.0
    for position, blocks in shards:
        heights = jax.random.uniform(jax.random.fold_in(jax.random.fold_in(rng, 6), position), (blocks,), jnp.float32, least / len(shards), largest / len(shards))
        factor_of = factor_of * jnp.repeat(jnp.exp(heights), dims[position] // blocks).reshape((-1,) + (1,) * (len(dims) - 1 - position))
    return factor_of


def profile(number_of, total, limit, lean):
    portions = [(1 << 20) // math.isqrt(rank ** lean) + 1 for rank in range(2, number_of + 1)]
    spare, counts = total - limit - (number_of - 1), [1] * (number_of - 1)
    while spare > 0:
        candidates = [i for i in range(number_of - 1) if counts[i] < limit]
        whole, budget = sum([portions[i] for i in candidates]), spare
        for i in candidates:
            more = min(limit - counts[i], max(1, budget * portions[i] // whole), spare)
            counts[i] = counts[i] + more
            spare = spare - more
    return np.array([limit] + counts)


def uneven_parts(own_key, count, total, bound, skew):
    if count == 2:
        one = jax.random.randint(own_key, (), max(1, total - bound), min(bound, total - 1) + 1)
        return jnp.stack([one, total - one])
    tallies = jnp.asarray(profile(count, total, bound, skew), jnp.int32)
    twos = (count - 1) // 2
    source_of, sink = tallies[1:1 + 2 * twos:2], tallies[2:2 + 2 * twos:2]
    room = jnp.minimum(source_of - 1, bound - sink)
    shifted = jax.random.randint(jax.random.fold_in(own_key, 1), (twos,), 0, 1 << 20) % (room + 1)
    tallies = tallies.at[1:1 + 2 * twos:2].set(source_of - shifted).at[2:2 + 2 * twos:2].set(sink + shifted)
    return tallies[jax.random.permutation(jax.random.fold_in(own_key, 2), count)]


def bell_draw(rng, shape, scale, reach, cuts=(), kind=jnp.bfloat16):
    loudness = block_levels(rng, shape, cuts, -0.22, 0.18) if cuts else 1.0
    array = jax.random.normal(rng, shape, jnp.float32) * scale * loudness
    return jnp.minimum(jnp.maximum(array, -reach), reach).astype(kind)


def setup_inputs(seed: int = 0) -> dict:
    arg_keys = jax.random.split(jax.random.key(seed), 15)
    arrivals = draw_arrivals(jax.random.fold_in(arg_keys[14], 71), 0)
    fresh = draw_fresh(jax.random.fold_in(arg_keys[14], 71), 0)
    stash = draw_stash(jax.random.fold_in(arg_keys[14], 71), 0)
    returning = bell_draw(arg_keys[3], (SECTION_LAYERS, PACKS, ROW_TOKENS, MODEL_WIDTH), 1.0, 6.0, ((0, 2), (1, 4), (3, 4)))
    loss_grad = bell_draw(arg_keys[4], (TICKS, PACKS, ROW_TOKENS, MODEL_WIDTH), 1.0, 6.0, ((1, 4), (3, 4)))
    gain = jnp.clip(1.0 + 0.18 * jax.random.normal(arg_keys[5], (SECTION_LAYERS, MODEL_WIDTH), jnp.float32), 0.1, 1.9)
    query_weight = bell_draw(arg_keys[6], (SECTION_LAYERS, MODEL_WIDTH, QUERY_HEADS * HEAD_SIZE), MODEL_WIDTH ** -0.5, 0.09375, ((0, 2), (1, 4), (2, 4)))
    key_weight = bell_draw(arg_keys[7], (SECTION_LAYERS, MODEL_WIDTH, KEY_VALUE_HEADS * HEAD_SIZE), MODEL_WIDTH ** -0.5, 0.09375, ((0, 2), (1, 4), (2, 4)))
    value_weight = bell_draw(arg_keys[8], (SECTION_LAYERS, MODEL_WIDTH, KEY_VALUE_HEADS * HEAD_SIZE), MODEL_WIDTH ** -0.5, 0.09375, ((0, 2), (1, 4), (2, 4)))
    w_out = bell_draw(arg_keys[9], (SECTION_LAYERS, QUERY_HEADS * HEAD_SIZE, MODEL_WIDTH), (QUERY_HEADS * HEAD_SIZE) ** -0.5, 0.09375, ((0, 2), (1, 4), (2, 4)))
    plan = jax.vmap(lambda own: jax.random.permutation(own, PACKS))(jax.random.split(arg_keys[10], TICKS)).reshape((TICKS, PACKS)).astype(jnp.int32)
    fresh_docs = jax.vmap(lambda own: jnp.searchsorted(jnp.cumsum(uneven_parts(own, DOCS, ROW_TOKENS, DOC_MOST, 2)), jnp.arange(ROW_TOKENS), side="right"))(jax.random.split(arg_keys[11], TICKS * PACKS)).reshape((TICKS, PACKS, ROW_TOKENS)).astype(jnp.int32)
    arrival_docs = jax.vmap(lambda own: jnp.searchsorted(jnp.cumsum(uneven_parts(own, DOCS, ROW_TOKENS, DOC_MOST, 2)), jnp.arange(ROW_TOKENS), side="right"))(jax.random.split(arg_keys[12], SECTION_LAYERS * PACKS)).reshape((SECTION_LAYERS, PACKS, ROW_TOKENS)).astype(jnp.int32)
    stash_docs = jax.vmap(lambda own: jnp.searchsorted(jnp.cumsum(uneven_parts(own, DOCS, ROW_TOKENS, DOC_MOST, 2)), jnp.arange(ROW_TOKENS), side="right"))(jax.random.split(arg_keys[13], TICKS * SECTION_LAYERS * PACKS)).reshape((TICKS, SECTION_LAYERS, PACKS, ROW_TOKENS)).astype(jnp.int32)
    return dict(arrivals=arrivals, fresh=fresh, stash=stash, returning=returning, loss_grad=loss_grad, gain=gain, query_weight=query_weight, key_weight=key_weight, value_weight=value_weight, w_out=w_out, plan=plan, fresh_docs=fresh_docs, arrival_docs=arrival_docs, stash_docs=stash_docs)


norm_eps = 1e-05

def round_journey(values):
    return lax.optimization_barrier(values.astype(jnp.bfloat16)).astype(jnp.float32)

def normalize(hidden, gain_row):
    hidden_f = hidden.astype(jnp.float32)
    inverse = lax.rsqrt(lax.optimization_barrier(jnp.sum(hidden_f * hidden_f, axis=-1)) / MODEL_WIDTH + norm_eps)
    normed = (hidden_f * inverse[..., None] * gain_row).astype(jnp.bfloat16)
    return (hidden_f, inverse, normed)

def allowed_pairs(documents):
    same = documents[:, :, None] == documents[:, None, :]
    causal = jnp.arange(ROW_TOKENS)[:, None] >= jnp.arange(ROW_TOKENS)[None, :]
    return jnp.logical_and(same, causal[None])[:, None, None]

def attention_parts(normed, documents, query_weight, key_weight, value_weight):
    packed_rows = normed.shape[0]
    group_width = QUERY_HEADS // KEY_VALUE_HEADS
    flattened = normed.reshape(packed_rows * ROW_TOKENS, MODEL_WIDTH)
    query_rows = round_journey(jnp.dot(flattened, query_weight, preferred_element_type=jnp.float32)).reshape(packed_rows, ROW_TOKENS, KEY_VALUE_HEADS, group_width, HEAD_SIZE)
    heads_of_key = round_journey(jnp.dot(flattened, key_weight, preferred_element_type=jnp.float32)).reshape(packed_rows, ROW_TOKENS, KEY_VALUE_HEADS, HEAD_SIZE)
    heads_of_value = round_journey(jnp.dot(flattened, value_weight, preferred_element_type=jnp.float32)).reshape(packed_rows, ROW_TOKENS, KEY_VALUE_HEADS, HEAD_SIZE)
    scores = jnp.einsum('pikgd,pjkd->pkgij', query_rows, heads_of_key) * HEAD_SIZE ** (-0.5)
    raised = jnp.where(allowed_pairs(documents), jnp.exp(scores), 0.0)
    probs = raised / lax.optimization_barrier(jnp.sum(raised, axis=-1, keepdims=True))
    probs_half = round_journey(probs)
    return (query_rows, heads_of_key, heads_of_value, probs, probs_half)

def grouped_sum(left, right):
    left_groups = jnp.moveaxis(left, 1, 0)
    right_groups = jnp.moveaxis(right, 1, 0)

    def step(total, pair):
        part = jnp.dot(pair[0], pair[1].T, preferred_element_type=jnp.float32).astype(jnp.bfloat16)
        part = lax.optimization_barrier(part)
        return (total + part.astype(jnp.float32), None)
    start_total = jnp.zeros((left.shape[0], right.shape[0]), jnp.float32)
    total, unused_out = lax.scan(step, start_total, (left_groups, right_groups))
    return total

def forward_layer(hidden, documents, gain_row, query_weight, key_weight, value_weight, w_out):
    hidden_f, inverse, normed = normalize(hidden, gain_row)
    query_rows, heads_of_key, heads_of_value, probs, probs_half = attention_parts(normed, documents, query_weight, key_weight, value_weight)
    packed_rows = hidden.shape[0]
    mixed = jnp.einsum('pkgij,pjkd->pikgd', probs_half, heads_of_value).astype(jnp.bfloat16).reshape(packed_rows * ROW_TOKENS, QUERY_HEADS * HEAD_SIZE)
    update = jnp.dot(mixed, w_out, preferred_element_type=jnp.float32).reshape(packed_rows, ROW_TOKENS, MODEL_WIDTH)
    return (hidden_f + update).astype(jnp.bfloat16)

def backward_layer(hidden, documents, grad, gain_row, query_weight, key_weight, value_weight, w_out):
    hidden_f, inverse, normed = normalize(hidden, gain_row)
    query_rows, heads_of_key, heads_of_value, probs, probs_half = attention_parts(normed, documents, query_weight, key_weight, value_weight)
    packed_rows = hidden.shape[0]
    tokens = packed_rows * ROW_TOKENS
    group_width = QUERY_HEADS // KEY_VALUE_HEADS
    block = MODEL_WIDTH // N_TENSOR
    query_cols = QUERY_HEADS * HEAD_SIZE // N_TENSOR
    key_columns = KEY_VALUE_HEADS * HEAD_SIZE // N_TENSOR
    grad_flat = grad.reshape(tokens, MODEL_WIDTH)
    head_gradient = grouped_sum(grad_flat.reshape(tokens, N_TENSOR, block), w_out.reshape(QUERY_HEADS * HEAD_SIZE, N_TENSOR, block))
    head_gradient = round_journey(head_gradient).reshape(packed_rows, ROW_TOKENS, KEY_VALUE_HEADS, group_width, HEAD_SIZE)
    prob_grad = jnp.einsum('pikgd,pjkd->pkgij', head_gradient, heads_of_value)
    score_grad = round_journey(probs * (prob_grad - lax.optimization_barrier(jnp.sum(probs * prob_grad, axis=-1, keepdims=True))) * HEAD_SIZE ** (-0.5))
    query_grad = jnp.einsum('pkgij,pjkd->pikgd', score_grad, heads_of_key).astype(jnp.bfloat16).reshape(tokens, N_TENSOR, query_cols)
    key_grad = jnp.einsum('pkgij,pikgd->pjkd', score_grad, query_rows).astype(jnp.bfloat16).reshape(tokens, N_TENSOR, key_columns)
    value_grad = jnp.einsum('pkgij,pikgd->pjkd', probs_half, head_gradient).astype(jnp.bfloat16).reshape(tokens, N_TENSOR, key_columns)
    left = jnp.concatenate([query_grad, key_grad, value_grad], axis=-1)
    right = jnp.concatenate([query_weight.reshape(MODEL_WIDTH, N_TENSOR, query_cols), key_weight.reshape(MODEL_WIDTH, N_TENSOR, key_columns), value_weight.reshape(MODEL_WIDTH, N_TENSOR, key_columns)], axis=-1)
    normed_grad = grouped_sum(left, right)
    hidden_flat = hidden_f.reshape(tokens, MODEL_WIDTH)
    inverse_flat = inverse.reshape(tokens)
    scaled = normed_grad * gain_row
    row_dot = lax.optimization_barrier(jnp.sum(scaled * hidden_flat, axis=-1))
    result = grad_flat.astype(jnp.float32) + inverse_flat[:, None] * scaled - hidden_flat * (inverse_flat ** 3 * row_dot / MODEL_WIDTH)[:, None]
    gain_term = lax.optimization_barrier(jnp.sum(normed_grad * hidden_flat * inverse_flat[:, None], axis=0))
    return (result.astype(jnp.bfloat16).reshape(packed_rows, ROW_TOKENS, MODEL_WIDTH), gain_term)

def reference(arrivals, fresh, stash, returning, loss_grad, gain, query_weight, key_weight, value_weight, w_out, plan, fresh_docs, arrival_docs, stash_docs):
    layers = arrivals.shape[0]
    balanced = [fresh[tick][plan[tick]] for tick in range(TICKS)]
    balanced_docs = [fresh_docs[tick][plan[tick]] for tick in range(TICKS)]
    outgoing = [arrivals[section] for section in range(layers)]
    going_back = [returning[section] for section in range(layers)]
    gain_total = [jnp.zeros((MODEL_WIDTH,), jnp.float32) for section in range(layers)]
    for tick in range(TICKS):
        new_out = []
        new_back = []
        for section in range(layers):
            if section == 0:
                hidden = balanced[tick]
            else:
                hidden = outgoing[section - 1]
            if section > tick:
                documents = arrival_docs[section - tick - 1]
            else:
                documents = balanced_docs[tick - section]
            new_out.append(forward_layer(hidden, documents, gain[section], query_weight[section], key_weight[section], value_weight[section], w_out[section]))
            if section == layers - 1:
                grad = loss_grad[tick]
            else:
                grad = going_back[section + 1]
            back, term = backward_layer(stash[tick, section], stash_docs[tick, section], grad, gain[section], query_weight[section], key_weight[section], value_weight[section], w_out[section])
            new_back.append(back)
            gain_total[section] = gain_total[section] + term
        outgoing = new_out
        going_back = new_back
    gain_grad = jnp.stack(gain_total) / math.sqrt(TICKS * PACKS * ROW_TOKENS)
    return (jnp.stack(outgoing), jnp.stack(going_back), gain_grad)
```

```python
import math

import jax
import jax.numpy as jnp
from jax import lax
from jax.sharding import PartitionSpec as P

MODEL_WIDTH = 4096
QUERY_HEADS = 32
KEY_VALUE_HEADS = 8
HEAD_SIZE = 128
TICKS = 2
NORM_EPS = 1e-05
F32 = jnp.float32
BF16 = jnp.bfloat16


def exchange(block, axis, mask):
    count = lax.axis_size(axis)
    return lax.ppermute(block, axis, [(i, i ^ mask) for i in range(count)])


def shifted(value, axis, steps):
    count = lax.axis_size(axis)
    leading, last = (max(0, -steps), min(count, count - steps))
    return lax.ppermute(value, axis, [(source, source + steps) for source in range(leading, last)])


def document_mask(documents):
    length = documents.shape[-1]
    same = documents[:, None] == documents[None, :]
    causal = jnp.arange(length)[:, None] >= jnp.arange(length)[None, :]
    return jnp.logical_and(same, causal)[None, None]


def attention_probs(query_rows, key_rows, value_rows, documents, kv_heads):
    length = documents.shape[0]
    per_key = query_rows.shape[1] // (kv_heads * HEAD_SIZE)
    query_heads = query_rows.reshape(length, kv_heads, per_key, HEAD_SIZE)
    heads_of_key = key_rows.reshape(length, kv_heads, HEAD_SIZE)
    heads_of_value = value_rows.reshape(length, kv_heads, HEAD_SIZE)
    scores = jnp.einsum(
        "ikgd,jkd->kgij", query_heads, heads_of_key, preferred_element_type=F32
    ) * HEAD_SIZE ** (-0.5)
    raised = jnp.where(document_mask(documents), jnp.exp(scores), 0.0)
    probs = raised / jnp.sum(raised, axis=-1, keepdims=True)
    return (query_heads, heads_of_key, heads_of_value, probs, probs.astype(BF16))


def local(
    arrivals,
    fresh,
    stash,
    returning,
    loss_grad,
    gain,
    query_weight,
    key_weight,
    value_weight,
    w_out,
    plan,
    fresh_docs,
    arrival_docs,
    stash_docs,
):
    tensor_count = lax.axis_size("tensor")
    section_count = lax.axis_size("section")
    replicas = lax.axis_size("dp")
    tensor_pos = lax.axis_index("tensor")
    section_pos = lax.axis_index("section")
    replica_pos = lax.axis_index("dp")
    length, width = arrivals.shape[2:]
    heads_here = QUERY_HEADS // tensor_count
    group_width = QUERY_HEADS // KEY_VALUE_HEADS
    share_count = max(1, group_width // heads_here)
    bit_count = share_count.bit_length() - 1
    query_cols = heads_here * HEAD_SIZE
    key_cols = key_weight.shape[2]
    block_rows = query_weight.shape[1]
    relative = tensor_count == replicas
    shift = tensor_pos if relative else 0

    def gather_dp(weight):
        other = exchange(weight, "dp", 2)
        sibling = exchange(weight, "dp", 1)
        return [weight, sibling, other, exchange(other, "dp", 1)]

    def assemble(parts_list):
        cols = sum(parts[0].shape[1] for parts in parts_list)
        whole = jnp.zeros((block_rows * replicas, cols), BF16)
        for mask in range(replicas):
            row = (replica_pos ^ mask ^ shift) * block_rows
            col = 0
            for parts in parts_list:
                whole = lax.dynamic_update_slice(whole, parts[mask], (row, col))
                col += parts[mask].shape[1]
        return whole

    def gather(block):
        if not relative:
            return lax.all_gather(block, "tensor", axis=block.ndim - 1, tiled=True)
        return jnp.concatenate(
            [block] + [exchange(block, "tensor", mask) for mask in range(1, tensor_count)], -1
        )

    def product_scatter(left, right):
        contract = (((1,), (1,)), ((), ()))
        if not relative:
            part = lax.dot_general(right, left, contract, preferred_element_type=F32).astype(BF16)
            return lax.psum_scatter(part, "tensor", scatter_dimension=0, tiled=True).astype(F32).T
        parts = []
        for mask in (2, 3, 1, 0):
            rows = right[mask * block_rows : (mask + 1) * block_rows]
            part = lax.dot_general(left, rows, contract, preferred_element_type=F32).astype(BF16)
            parts.append(exchange(part, "tensor", mask) if mask else part)
        return sum(part.astype(F32) for part in parts)

    def sum_tensor(value):
        if not relative:
            return lax.psum(value, "tensor")
        return value + sum(exchange(value, "tensor", mask) for mask in range(1, tensor_count))

    def balance(rows, order):
        sibling = exchange(rows, "dp", 1)
        asked = order[replica_pos ^ 2]
        far = exchange(jnp.where(asked == replica_pos, rows, sibling), "dp", 2)
        source = order[replica_pos]
        return jnp.where(
            source == replica_pos, rows, jnp.where(source == replica_pos ^ 1, sibling, far)
        )

    fresh_rows = [balance(fresh[tick, 0], plan[tick]) for tick in range(TICKS)]
    fresh_documents = jnp.stack(
        [
            lax.dynamic_index_in_dim(fresh_docs[tick], plan[tick][replica_pos], 0, keepdims=False)
            for tick in range(TICKS)
        ]
    )
    gain_row = gain[0]
    gain_all = gather(gain)[0]
    out_w = assemble([gather_dp(w_out[0])])
    own_kv = jnp.stack([key_weight[0], value_weight[0]])
    for bit in range(bit_count):
        partner = exchange(own_kv, "tensor", 1 << bit)
        low_side = tensor_pos >> bit & 1 == 0
        own_kv = jnp.where(
            low_side,
            jnp.concatenate([own_kv, partner], -1),
            jnp.concatenate([partner, own_kv], -1),
        )
    query_parts = gather_dp(query_weight[0])
    forward_w = assemble([query_parts, gather_dp(own_kv[0]), gather_dp(own_kv[1])])
    if bit_count:
        grad_w = assemble([query_parts, gather_dp(key_weight[0]), gather_dp(value_weight[0])])
    else:
        grad_w = forward_w
    head_cols = own_kv.shape[2]

    def project(hidden_rows):
        hidden_f = hidden_rows.astype(F32)
        inverse = lax.rsqrt(jnp.sum(hidden_f * hidden_f, -1) / MODEL_WIDTH + NORM_EPS)
        product = jnp.dot(
            (hidden_f * gain_all).astype(BF16), forward_w, preferred_element_type=F32
        )
        return inverse, (product * inverse[:, None]).astype(BF16)

    def split(rows):
        return (
            rows[:, :query_cols],
            rows[:, query_cols : query_cols + head_cols],
            rows[:, query_cols + head_cols :],
        )

    kv_heads = head_cols // HEAD_SIZE

    def forward(hidden, documents, projected):
        parts = attention_probs(*split(projected), documents, kv_heads)
        mixed = jnp.einsum("kgij,jkd->ikgd", parts[4], parts[2], preferred_element_type=F32)
        mixed = mixed.astype(BF16).reshape(length, query_cols)
        attended = jnp.dot(gather(mixed), out_w, preferred_element_type=F32)
        return (hidden.astype(F32) + attended).astype(BF16)

    def backward(hidden, documents, grad, inverse, projected):
        query_heads, heads_of_key, heads_of_value, probs, probs_half = attention_probs(
            *split(projected), documents, kv_heads
        )
        head_gradient = product_scatter(grad, out_w).astype(BF16).reshape(query_heads.shape)
        prob_grad = jnp.einsum(
            "ikgd,jkd->kgij", head_gradient, heads_of_value, preferred_element_type=F32
        )
        score_grad = (
            probs
            * (prob_grad - jnp.sum(probs * prob_grad, axis=-1, keepdims=True))
            * HEAD_SIZE ** (-0.5)
        ).astype(BF16)
        query_grad = jnp.einsum(
            "kgij,jkd->ikgd", score_grad, heads_of_key, preferred_element_type=F32
        )
        query_grad = query_grad.astype(BF16).reshape(length, query_cols)
        key_grad = jnp.einsum(
            "kgij,ikgd->jkd", score_grad, query_heads, preferred_element_type=F32
        ).reshape(length, -1)
        value_grad = jnp.einsum(
            "kgij,ikgd->jkd", probs_half, head_gradient, preferred_element_type=F32
        ).reshape(length, -1)
        grads = jnp.concatenate([query_grad.astype(F32), key_grad, value_grad], 1)
        row_dot = sum_tensor(jnp.sum(grads * projected.astype(F32), -1)) / inverse
        kv_grad = jnp.stack([key_grad, value_grad])
        for bit in reversed(range(bit_count)):
            half = kv_grad.shape[-1] // 2
            low_side = tensor_pos >> bit & 1 == 0
            keep = jnp.where(low_side, kv_grad[..., :half], kv_grad[..., half:])
            outward = jnp.where(low_side, kv_grad[..., half:], kv_grad[..., :half])
            kv_grad = keep + exchange(outward.astype(BF16), "tensor", 1 << bit).astype(F32)
        kv_grad = kv_grad.astype(BF16)
        grad_rows = jnp.concatenate([query_grad, kv_grad[0], kv_grad[1]], axis=1)
        normed_grad = product_scatter(grad_rows, grad_w)
        hidden_f = hidden.astype(F32)
        result = (
            grad.astype(F32)
            + inverse[:, None] * (normed_grad * gain_row)
            - hidden_f * (inverse**3 * row_dot / MODEL_WIDTH)[:, None]
        )
        term = jnp.sum(normed_grad * hidden_f * inverse[:, None], axis=0)
        return result.astype(BF16), term

    outgoing = arrivals[0, 0]
    going_back = returning[0, 0]
    saved = [project(gather(stash[tick, 0, 0])) for tick in range(TICKS)]
    gain_total = jnp.zeros((width,), F32)
    for tick in range(TICKS):
        forward_in = jnp.where(section_pos == 0, fresh_rows[tick], shifted(outgoing, "section", 1))
        from_arrivals = lax.dynamic_index_in_dim(
            arrival_docs, jnp.clip(section_pos - tick - 1, 0, section_count - 1), 0, keepdims=False
        )[0]
        from_fresh = lax.dynamic_index_in_dim(
            fresh_documents, jnp.clip(tick - section_pos, 0, TICKS - 1), 0, keepdims=False
        )
        forward_docs = jnp.where(section_pos > tick, from_arrivals, from_fresh)
        grad_in = jnp.where(
            section_pos == section_count - 1,
            loss_grad[tick, 0],
            shifted(going_back, "section", -1),
        )
        outgoing = forward(forward_in, forward_docs, project(gather(forward_in))[1])
        going_back, term = backward(
            stash[tick, 0, 0], stash_docs[tick, 0, 0], grad_in, *saved[tick]
        )
        gain_total = gain_total + term
    gain_total = gain_total + exchange(gain_total, "dp", 1)
    gain_total = gain_total + exchange(gain_total, "dp", 2)
    gain_grad = gain_total / math.sqrt(TICKS * replicas * length)
    return (outgoing[None, None], going_back[None, None], gain_grad[None])


def solution(mesh):
    return jax.shard_map(
        local,
        mesh=mesh,
        in_specs=(
            P("section", "dp", None, "tensor"),
            P(None, "dp", None, "tensor"),
            P(None, "section", "dp", None, "tensor"),
            P("section", "dp", None, "tensor"),
            P(None, "dp", None, "tensor"),
            P("section", "tensor"),
            P("section", "dp", "tensor"),
            P("section", "dp", "tensor"),
            P("section", "dp", "tensor"),
            P("section", "dp", "tensor"),
            P(),
            P(),
            P(None, "dp", None),
            P(None, "section", "dp", None),
        ),
        out_specs=(
            P("section", "dp", None, "tensor"),
            P("section", "dp", None, "tensor"),
            P("section", "tensor"),
        ),
        check_vma=False,
    )
```

```python
import functools
import math

import jax
import jax.numpy as jnp
from jax import lax
from jax.experimental import pallas as pl
from jax.experimental.pallas import tpu as pltpu
from jax.sharding import PartitionSpec as P

MODEL_WIDTH = 4096
QUERY_HEADS = 32
KEY_VALUE_HEADS = 8
HEAD_SIZE = 128
TICKS = 2
NORM_EPS = 1e-05
F32 = jnp.float32
BF16 = jnp.bfloat16


NEAR = (((1,), (1,)), ((), ()))
FIRST = (((0,), (0,)), ((), ()))
CHUNKS = 2
VMEM = 32 * 2**20


def exchange(block, axis, mask):
    count = lax.axis_size(axis)
    return lax.ppermute(block, axis, [(i, i ^ mask) for i in range(count)])


def shifted(value, axis, steps):
    count = lax.axis_size(axis)
    leading, last = (max(0, -steps), min(count, count - steps))
    return lax.ppermute(value, axis, [(source, source + steps) for source in range(leading, last)])


def dot(left, right, contract=(((1,), (0,)), ((), ()))):
    return lax.dot_general(left, right, contract, preferred_element_type=F32)


def call(kernel, args, outs, scratch=(), specs=None, after=()):

    def whole(dims):
        return pl.BlockSpec(dims, lambda step: (0,) * len(dims))

    def body(*refs):
        kernel(*refs[: len(args)], *refs[len(args) + len(after) :])

    return pl.pallas_call(
        body,
        grid=(1,),
        in_specs=[
            spec if spec is not None else whole(a.shape)
            for spec, a in zip(specs or [None] * len(args), args)
        ]
        + [pl.BlockSpec(memory_space=pl.ANY)] * len(after),
        out_specs=[whole(o.shape) for o in outs],
        out_shape=[jax.ShapeDtypeStruct(o.shape, o.dtype) for o in outs],
        scratch_shapes=list(scratch),
        compiler_params=pltpu.CompilerParams(vmem_limit_bytes=VMEM),
        cost_estimate=pl.CostEstimate(flops=1024, bytes_accessed=1024, transcendentals=0),
    )(*args, *after)


def tie(value, *after):
    def body(*refs):
        pass

    return pl.pallas_call(
        body,
        in_specs=[pl.BlockSpec(memory_space=pl.ANY)] * (1 + len(after)),
        out_specs=pl.BlockSpec(memory_space=pl.ANY),
        out_shape=jax.ShapeDtypeStruct(value.shape, value.dtype),
        input_output_aliases={0: 0},
        cost_estimate=pl.CostEstimate(flops=0, bytes_accessed=0, transcendentals=0),
    )(value, *after)


def shape(rows, cols, dtype=F32):
    return jax.ShapeDtypeStruct((rows, cols), dtype)


class Loader:
    def __init__(self, which_ref, groups, buffers, sems, count):
        self.groups, self.buffers, self.sems = groups, buffers, sems
        for i in range(count):
            for chunk in range(CHUNKS):
                for group, parts in enumerate(groups):
                    for k, part in enumerate(parts):
                        pl.when(which_ref[i] == k)(self.copy(part, group, i, chunk).start)

    def copy(self, part, group, i, chunk):
        rows = part.shape[0] // CHUNKS
        at = pl.ds(chunk * rows, rows)
        return pltpu.make_async_copy(
            part.at[at], self.buffers[group].at[i, at], self.sems.at[group, i, chunk]
        )

    def wait(self, group, i, chunk):
        self.copy(self.groups[group][0], group, i, chunk).wait()


def load_scratch(groups, count):
    return [pltpu.VMEM((count,) + parts[0].shape, BF16) for parts in groups] + [
        pltpu.SemaphoreType.DMA((len(groups), count, CHUNKS))
    ]


def sum_kernel(count, sizes, has_gains, has_before, final, *refs):
    refs = list(refs)
    take = lambda n: [refs.pop(0) for _ in range(n)]
    (which,) = take(1)
    blocks = take(count)
    gains = take(count) if has_gains else []
    groups = [take(size) for size in sizes]
    totals_in = take(len(sizes) + has_gains) if has_before else []
    hidden = take(1) if final else []
    totals = take(len(sizes) + has_gains)
    loader = Loader(which, groups, take(len(sizes)), refs.pop(), count)
    squares = totals_in[-1][...] if has_gains and has_before else 0.0
    running = {}
    for i in range(count):
        block = blocks[i][...]
        if has_gains:
            block = block.astype(F32)
            squares = squares + jnp.sum(block * block, axis=-1, keepdims=True)
            block = (block * gains[i][...]).astype(BF16)
        rows = block.shape[1] // CHUNKS
        for chunk in range(CHUNKS):
            for group in range(len(sizes)):
                loader.wait(group, i, chunk)
                at = slice(chunk * rows, (chunk + 1) * rows)
                term = dot(block[:, at], loader.buffers[group][i, at])
                if i or chunk:
                    term = term + running[group]
                elif has_before:
                    term = term + totals_in[group][...]
                running[group] = term
    for group in range(len(sizes)):
        if final:
            totals[group][...] = (running[group] + hidden[0][...].astype(F32)).astype(BF16)
        else:
            totals[group][...] = running[group]
    if has_gains:
        totals[-1][...] = squares


def sum_of(which, blocks, groups, gains=(), before=(), hidden=None, after=()):
    length = blocks[0].shape[0]
    args = [which, *blocks, *gains]
    specs = [pl.BlockSpec(memory_space=pltpu.SMEM)] + [None] * (len(args) - 1)
    for parts in groups:
        args += parts
        specs += [pl.BlockSpec(memory_space=pl.ANY)] * len(parts)
    args += [*before] + ([] if hidden is None else [hidden])
    specs += [None] * (len(args) - len(specs))
    outs = [
        shape(length, parts[0].shape[1], F32 if hidden is None else BF16) for parts in groups
    ] + ([shape(length, 1)] if gains else [])
    return call(
        functools.partial(
            sum_kernel,
            len(blocks),
            [len(parts) for parts in groups],
            bool(gains),
            bool(before),
            hidden is not None,
        ),
        args,
        outs,
        load_scratch(groups, len(blocks)),
        specs,
        after,
    )


def turned_kernel(sizes, count, has_aside, *refs):
    refs = list(refs)
    take = lambda n: [refs.pop(0) for _ in range(n)]
    (which,) = take(1)
    lefts = take(len(sizes))
    groups = [take(size) for size in sizes]
    aside = take(1) if has_aside else []
    outs = take(count)
    loader = Loader(which, groups, take(len(sizes)), refs.pop(), count)
    width = groups[0][0].shape[0]
    rows = width // CHUNKS
    for i, out in enumerate(outs):
        for chunk in range(CHUNKS):
            at = slice(chunk * rows, (chunk + 1) * rows)
            total = 0.0
            for group, left in enumerate(lefts):
                loader.wait(group, i, chunk)
                total = total + dot(left[...], loader.buffers[group][i, at], NEAR)
            out[:, at] = total.astype(out.dtype)
    if has_aside:
        outs[0][:, width:] = aside[0][...]


def turned_products(which, lefts, groups, dtypes, aside=None, after=()):
    args = [which, *lefts]
    specs = [pl.BlockSpec(memory_space=pltpu.SMEM)] + [None] * len(lefts)
    for parts in groups:
        args += parts
        specs += [pl.BlockSpec(memory_space=pl.ANY)] * len(parts)
    args += [] if aside is None else [aside]
    specs += [None] * (len(args) - len(specs))
    width = groups[0][0].shape[0]
    outs = [shape(lefts[0].shape[0], width, dtype) for dtype in dtypes]
    if aside is not None:
        outs[0] = shape(lefts[0].shape[0], width + aside.shape[1], dtypes[0])
    return call(
        functools.partial(
            turned_kernel, [len(parts) for parts in groups], len(dtypes), aside is not None
        ),
        args,
        outs,
        load_scratch(groups, len(dtypes)),
        specs,
        after,
    )


def joined_kernel(part_ref, last_ref, *refs):
    out = refs[-1]
    width = part_ref.shape[1]
    out[:, :width] = (part_ref[...] + last_ref[:, :width].astype(F32)).astype(BF16)
    if len(refs) > 1:
        value = refs[0][...].astype(F32) + last_ref[:, width:].astype(F32)
        out[:, width:] = two_lanes(value[:, :1] + value[:, 1:2], value.shape)


def two_lanes(value, dims):
    high = value.astype(BF16).astype(F32)
    lane = lax.broadcasted_iota(jnp.int32, dims, 1)
    return jnp.where(lane == 0, high, jnp.where(lane == 1, value - high, 0.0)).astype(BF16)


def stacked(value, first, per_key):
    return jnp.concatenate(
        [value[:, (first + a) * HEAD_SIZE : (first + a + 1) * HEAD_SIZE] for a in range(per_key)], 0
    )


def masked_probs(rows, keys, docs_down, docs_across, per_key):
    length = keys.shape[0]
    scores = dot(rows, keys, NEAR) * HEAD_SIZE ** (-0.5)
    down = lax.broadcasted_iota(jnp.int32, (length, length), 0)
    across = lax.broadcasted_iota(jnp.int32, (length, length), 1)
    allowed = jnp.logical_and(docs_down[...] == docs_across[...], down >= across)
    allowed = jnp.concatenate([allowed.astype(F32)] * per_key, 0) > 0.5
    raised = jnp.where(allowed, jnp.exp(scores), 0.0)
    return raised / jnp.sum(raised, axis=-1, keepdims=True)


def normed_rows(query_ref, kv_ref, squares_ref):
    inverse = lax.rsqrt(squares_ref[...] / MODEL_WIDTH + NORM_EPS)
    return (query_ref[...] * inverse).astype(BF16), (kv_ref[...] * inverse).astype(BF16)


def forward_heads(kv_heads, query_ref, kv_ref, squares_ref, down_ref, across_ref, mixed_ref):
    length, query_cols = mixed_ref.shape
    per_key = query_cols // (kv_heads * HEAD_SIZE)
    queries, kv = normed_rows(query_ref, kv_ref, squares_ref)
    for head in range(kv_heads):
        key_at = head * HEAD_SIZE
        value_at = key_at + kv_heads * HEAD_SIZE
        query = stacked(queries, head * per_key, per_key)
        keys = kv[:, key_at : key_at + HEAD_SIZE]
        probs = masked_probs(query, keys, down_ref, across_ref, per_key)
        mixed = dot(probs.astype(BF16), kv[:, value_at : value_at + HEAD_SIZE]).astype(BF16)
        for a in range(per_key):
            at = (head * per_key + a) * HEAD_SIZE
            mixed_ref[:, at : at + HEAD_SIZE] = mixed[a * length : (a + 1) * length]


def backward_heads(kv_heads, count, rows_ref, kv_rows_ref, squares_ref, down_ref, across_ref, *refs):
    terms, (query_ref, kv_ref, dot_ref) = refs[:count], refs[count:]
    length, query_cols = query_ref.shape
    per_key = query_cols // (kv_heads * HEAD_SIZE)
    queries, kv = normed_rows(rows_ref, kv_rows_ref, squares_ref)
    total = terms[0][...].astype(F32)
    for term in terms[1:]:
        total = total + term[...].astype(F32)
    grads = total.astype(BF16)
    row_dot = jnp.zeros((length, 1), F32)
    for head in range(kv_heads):
        key_at = head * HEAD_SIZE
        value_at = key_at + kv_heads * HEAD_SIZE
        query = stacked(queries, head * per_key, per_key)
        keys = kv[:, key_at : key_at + HEAD_SIZE]
        values = kv[:, value_at : value_at + HEAD_SIZE]
        probs = masked_probs(query, keys, down_ref, across_ref, per_key)
        grad = stacked(grads, head * per_key, per_key)
        prob_grad = dot(grad, values, NEAR)
        inner = jnp.sum(probs * prob_grad, axis=-1, keepdims=True)
        score_grad = (probs * (prob_grad - inner) * HEAD_SIZE ** (-0.5)).astype(BF16)
        query_grad = dot(score_grad, keys)
        key_grad = dot(score_grad, query, FIRST)
        value_grad = dot(probs.astype(BF16), grad, FIRST)
        products = jnp.sum(query_grad * query.astype(F32), axis=-1, keepdims=True)
        for a in range(per_key):
            at = (head * per_key + a) * HEAD_SIZE
            rows = slice(a * length, (a + 1) * length)
            query_ref[:, at : at + HEAD_SIZE] = query_grad[rows].astype(BF16)
            row_dot = row_dot + products[rows]
        row_dot = row_dot + jnp.sum(key_grad * keys.astype(F32), axis=-1, keepdims=True)
        row_dot = row_dot + jnp.sum(value_grad * values.astype(F32), axis=-1, keepdims=True)
        kv_ref[:, key_at : key_at + HEAD_SIZE] = key_grad.astype(kv_ref.dtype)
        kv_ref[:, value_at : value_at + HEAD_SIZE] = value_grad.astype(kv_ref.dtype)
    dot_ref[...] = two_lanes(row_dot, dot_ref.shape)


def split_float(value):
    high = lax.reduce_precision(value, 8, 7)
    middle = lax.reduce_precision(value - high, 8, 7)
    return [high.astype(BF16), middle.astype(BF16), (value - high - middle).astype(BF16)]


def local(
    arrivals,
    fresh,
    stash,
    returning,
    loss_grad,
    gain,
    query_weight,
    key_weight,
    value_weight,
    w_out,
    plan,
    fresh_docs,
    arrival_docs,
    stash_docs,
):
    tensor_count = lax.axis_size("tensor")
    section_count = lax.axis_size("section")
    replicas = lax.axis_size("dp")
    tensor_pos = lax.axis_index("tensor")
    section_pos = lax.axis_index("section")
    replica_pos = lax.axis_index("dp")
    length, width = arrivals.shape[2:]
    heads_here = QUERY_HEADS // tensor_count
    group_width = QUERY_HEADS // KEY_VALUE_HEADS
    share_count = max(1, group_width // heads_here)
    bit_count = share_count.bit_length() - 1
    query_cols = heads_here * HEAD_SIZE
    block_rows = query_weight.shape[1]
    relative = tensor_count == replicas
    shift = tensor_pos if relative else 0
    which = [(replica_pos ^ mask ^ shift).astype(jnp.int32) for mask in range(replicas)]

    def picks(*masks):
        return jnp.stack([which[mask] for mask in masks])

    def fixed(*masks):
        return jnp.array(masks, jnp.int32)

    def gather_dp(weight):
        other = exchange(weight, "dp", 2)
        sibling = exchange(weight, "dp", 1)
        return [weight, sibling, other, exchange(other, "dp", 1)]

    def gather(block):
        if not relative:
            whole = lax.all_gather(block, "tensor", axis=1, tiled=True)
            return jnp.split(whole, replicas, 1)
        far = exchange(block, "tensor", 2)
        near = exchange(block, "tensor", 1)
        return [block, near, far, exchange(far, "tensor", 1)]

    def product_scatter(lefts, groups, aside=None, after=()):
        if not relative:
            part = turned_products(picks(0, 1, 2, 3), lefts, groups, [BF16] * 4)
            part = jnp.concatenate(part, 1)
            terms = [lax.psum_scatter(part, "tensor", scatter_dimension=1, tiled=True)]
            if aside is None:
                return terms
            return terms, lax.psum(aside[:, :1].astype(F32) + aside[:, 1:2].astype(F32), "tensor")
        (last,) = turned_products(picks(3), lefts, groups, [BF16], aside, after)
        near, far = turned_products(picks(1, 2), lefts, groups, [BF16, F32], None, [last])
        last = exchange(last, "tensor", 1)
        near = exchange(near, "tensor", 1)
        asides = [] if aside is None else [aside]
        (joined,) = call(
            joined_kernel, [far, last, *asides], [shape(length, last.shape[1], BF16)]
        )
        far = exchange(joined, "tensor", 2)
        (own,) = turned_products(picks(0), lefts, groups, [BF16], None, [joined])
        terms = [own, near, far[:, :block_rows]]
        if aside is None:
            return terms
        sides = [aside, last[:, block_rows:], far[:, block_rows:]]
        return terms, sum(
            side[:, i : i + 1].astype(F32) for side in sides for i in range(2)
        )

    def balance(rows):
        sibling = exchange(rows, "dp", 1)
        asked = plan[:, replica_pos ^ 2][:, None, None]
        source = plan[:, replica_pos][:, None, None]
        far = exchange(jnp.where(asked == replica_pos, rows, sibling), "dp", 2)
        return jnp.where(
            source == replica_pos, rows, jnp.where(source == replica_pos ^ 1, sibling, far)
        )

    balanced = balance(fresh[:, 0])
    own_kv = [key_weight[0], value_weight[0]]
    pair_kv = own_kv
    for bit in range(bit_count):
        low_side = tensor_pos >> bit & 1 == 0
        partners = [exchange(block, "tensor", 1 << bit) for block in pair_kv]
        pair_kv = [
            jnp.where(
                low_side,
                jnp.concatenate([block, partner], -1),
                jnp.concatenate([partner, block], -1),
            )
            for block, partner in zip(pair_kv, partners)
        ]
    head_cols = pair_kv[0].shape[1]
    kv_heads = head_cols // HEAD_SIZE
    kv_weight = jnp.concatenate(pair_kv, 1)
    out_x, kv_x, query_x = [
        exchange(weight, "dp", 2) for weight in (w_out[0], kv_weight, query_weight[0])
    ]
    out_sibling, kv_sibling, query_sibling = [
        exchange(weight, "dp", 1) for weight in (w_out[0], kv_weight, query_weight[0])
    ]

    def far_dp(weight, sibling, other):
        return [weight, sibling, other, exchange(other, "dp", 1)]

    gain_row = gain[0]

    def attend(kernel, outs, sums, group, documents, terms=(), after=()):
        row = [pl.BlockSpec((length, a.shape[1]), lambda step: (group, 0)) for a in sums]
        args = (*sums, documents[:, None], documents[None, :], *terms)
        return call(kernel, args, outs, (), row + [None] * (2 + len(terms)), after)

    def mix(documents, sums, group):
        (mixed,) = attend(
            functools.partial(forward_heads, kv_heads),
            [shape(length, query_cols, BF16)],
            sums,
            group,
            documents,
        )
        return mixed

    def project_out(hidden, blocks, after=()):
        before = sum_of(picks(0, 1, 2), blocks[:3], [out_parts], after=after)
        return sum_of(picks(3), blocks[3:], [out_parts], (), before, hidden)[0]

    def head_terms(grad, after=()):
        return product_scatter([grad], [out_parts], None, after)

    def backward(hidden, documents, grad, terms, sums, group, after=()):
        query_grad, kv_grad, aside = attend(
            functools.partial(backward_heads, kv_heads, len(terms)),
            [
                shape(length, query_cols, BF16),
                shape(length, 2 * head_cols, F32 if bit_count else BF16),
                shape(length, HEAD_SIZE, BF16),
            ],
            sums,
            group,
            documents,
            terms,
            after,
        )
        if bit_count:
            kv_grad = jnp.stack([kv_grad[:, :head_cols], kv_grad[:, head_cols:]])
            for bit in reversed(range(bit_count)):
                half = kv_grad.shape[-1] // 2
                low_side = tensor_pos >> bit & 1 == 0
                keep = jnp.where(low_side, kv_grad[..., :half], kv_grad[..., half:])
                outward = jnp.where(low_side, kv_grad[..., half:], kv_grad[..., :half])
                kv_grad = keep + exchange(outward.astype(BF16), "tensor", 1 << bit).astype(F32)
            kv_grad = jnp.concatenate([kv_grad[0], kv_grad[1]], 1).astype(BF16)
        terms, row_dot = product_scatter(
            [query_grad, kv_grad], [query_parts, grad_kv_parts], aside
        )
        normed_grad = sum(term.astype(F32) for term in terms)
        squares = sums[2][group * length : (group + 1) * length]
        inverse = lax.rsqrt(squares / MODEL_WIDTH + NORM_EPS)
        row_dot = row_dot / inverse
        hidden_f = hidden.astype(F32)
        result = (
            grad.astype(F32)
            + inverse * (normed_grad * gain_row)
            - hidden_f * (inverse**3 * row_dot / MODEL_WIDTH)
        )
        term = jnp.sum(normed_grad * hidden_f * inverse, axis=0)
        return result.astype(BF16), term

    def forward_documents(tick):
        from_arrivals = lax.dynamic_index_in_dim(
            arrival_docs, jnp.clip(section_pos - tick - 1, 0, section_count - 1), 0, keepdims=False
        )[0]
        step = jnp.clip(tick - section_pos, 0, TICKS - 1)
        from_fresh = fresh_docs[step, plan[step, replica_pos]]
        return jnp.where(section_pos > tick, from_arrivals, from_fresh)

    first_in = balanced[0]
    if section_count > TICKS:
        first_in = jnp.where(section_pos == 0, first_in, shifted(arrivals[0, 0], "section", 1))
    grad_in = jnp.where(
        section_pos == section_count - 1,
        loss_grad[0, 0],
        shifted(returning[0, 0], "section", -1),
    )
    gain_rows = jnp.stack(split_float(gain_row) + [jnp.zeros((width,), BF16)] * 13)
    early = jnp.concatenate([stash[0, 0, 0], stash[1, 0, 0], gain_rows], 0)
    early = lax.all_gather(early, "tensor")
    first_in = tie(first_in, out_x, kv_x)
    firsts = jnp.stack(gather(first_in))

    def early_block(index):
        group = tensor_count // replicas
        block = lax.dynamic_slice_in_dim(early, index * group, group, 0)
        return block.transpose(1, 0, 2).reshape(early.shape[1], block_rows)

    def gain_of(block):
        return sum(block[-16 + i : -15 + i].astype(F32) for i in range(3))

    saved = TICKS * length
    squares = jnp.sum(jnp.square(early[:, :saved].astype(F32)), (0, 2))
    squares = jnp.concatenate([squares, jnp.sum(jnp.square(firsts.astype(F32)), (0, 2))])[:, None]
    rows = []
    for mask in range(replicas):
        block = early_block(replica_pos ^ mask)
        first = lax.dynamic_index_in_dim(firsts, which[mask], 0, keepdims=False)
        row = jnp.concatenate([block[:saved], first], 0).astype(F32) * gain_of(block)
        rows.append(row.astype(BF16))
    gains = [gain_of(early_block(mask ^ shift)) for mask in range(replicas)]
    out_parts = far_dp(w_out[0], out_sibling, out_x)
    kv_parts = far_dp(kv_weight, kv_sibling, kv_x)
    terms = head_terms(grad_in)
    (kv_sum,) = sum_of(fixed(0, 1, 2, 3), rows, [kv_parts])
    query_early = [query_weight[0], query_sibling]
    query_sum = sum_of(fixed(0, 1), rows[:2], [query_early])
    query_x = tie(query_x, kv_sum, *query_sum, *terms)
    query_parts = far_dp(query_weight[0], query_sibling, query_x)
    query_sum = sum_of(fixed(0), rows[2:3], [query_parts[2:3]], (), query_sum)
    query_sum = sum_of(fixed(0), rows[3:], [query_parts[3:]], (), query_sum)
    sums = [*query_sum, kv_sum, squares]
    if bit_count:
        grad_kv_parts = gather_dp(jnp.concatenate(own_kv, 1))
    else:
        grad_kv_parts = kv_parts

    mixed = mix(forward_documents(0), sums, TICKS)
    blocks = gather(mixed)
    going_back, gain_total = backward(
        stash[0, 0, 0], stash_docs[0, 0, 0], grad_in, terms, sums, 0, [mixed]
    )
    outgoing = project_out(first_in, blocks)
    forward_in = jnp.where(section_pos == 0, balanced[1], shifted(outgoing, "section", 1))
    grad_in = jnp.where(
        section_pos == section_count - 1, loss_grad[1, 0], shifted(going_back, "section", -1)
    )
    blocks = gather(forward_in)
    groups = [query_parts, kv_parts]
    terms = head_terms(grad_in, [forward_in])
    later = sum_of(picks(0, 1, 2), blocks[:3], groups, gains[:3])
    later = sum_of(picks(3), blocks[3:], groups, gains[3:], later)
    mixed = mix(forward_documents(1), later, 0)
    blocks = gather(mixed)
    going_back, term = backward(
        stash[1, 0, 0], stash_docs[1, 0, 0], grad_in, terms, sums, 1, [mixed]
    )
    outgoing = project_out(forward_in, blocks)
    gain_total = gain_total + term
    gain_total = gain_total + exchange(gain_total, "dp", 1)
    gain_total = gain_total + exchange(gain_total, "dp", 2)
    gain_grad = gain_total / math.sqrt(TICKS * replicas * length)
    return (outgoing[None, None], going_back[None, None], gain_grad[None])


def solution(mesh):
    return jax.shard_map(
        local,
        mesh=mesh,
        in_specs=(
            P("section", "dp", None, "tensor"),
            P(None, "dp", None, "tensor"),
            P(None, "section", "dp", None, "tensor"),
            P("section", "dp", None, "tensor"),
            P(None, "dp", None, "tensor"),
            P("section", "tensor"),
            P("section", "dp", "tensor"),
            P("section", "dp", "tensor"),
            P("section", "dp", "tensor"),
            P("section", "dp", "tensor"),
            P(),
            P(),
            P(None, "dp", None),
            P(None, "section", "dp", None),
        ),
        out_specs=(
            P("section", "dp", None, "tensor"),
            P("section", "dp", None, "tensor"),
            P("section", "tensor"),
        ),
        check_vma=False,
    )
```

```python
import functools
import math

import jax
import jax.numpy as jnp
from jax import lax
from jax.experimental import pallas as pl
from jax.experimental.pallas import tpu as pltpu
from jax.sharding import PartitionSpec as P

MODEL_WIDTH = 4096
QUERY_HEADS = 32
KEY_VALUE_HEADS = 8
HEAD_SIZE = 128
TICKS = 2
NORM_EPS = 1e-05
F32 = jnp.float32
BF16 = jnp.bfloat16


NEAR = (((1,), (1,)), ((), ()))
FIRST = (((0,), (0,)), ((), ()))
CHUNKS = 2
VMEM = 22 * 2**20
SMEM_SPEC = pl.BlockSpec(memory_space=pltpu.SMEM)
ANY_SPEC = pl.BlockSpec(memory_space=pl.ANY)
VMEM_SPEC = pl.BlockSpec(memory_space=pltpu.VMEM)


def exchange(block, axis, mask):
    count = lax.axis_size(axis)
    return lax.ppermute(block, axis, [(i, i ^ mask) for i in range(count)])


def exchange_tensor(block, mask, sections):
    count = lax.axis_size("tensor")
    return lax.ppermute(
        block,
        ("section", "tensor"),
        [(s * count + i, s * count + (i ^ mask)) for s in sections for i in range(count)],
    )


def shifted(value, axis, steps):
    count = lax.axis_size(axis)
    leading, last = (max(0, -steps), min(count, count - steps))
    return lax.ppermute(value, axis, [(source, source + steps) for source in range(leading, last)])


def dot(left, right, contract=(((1,), (0,)), ((), ()))):
    return lax.dot_general(left, right, contract, preferred_element_type=F32)


def shape(rows, cols, dtype=F32):
    return jax.ShapeDtypeStruct((rows, cols), dtype)


class Work:
    def __init__(self, body, args, groups=(), which=None):
        self.body, self.groups = body, groups
        self.count = 0 if which is None else which.shape[0]
        pairs = [arg if isinstance(arg, tuple) else (arg, ()) for arg in args]
        self.index = [index for _, index in pairs]
        self.plain = len(args)
        self.args = [array for array, _ in pairs] + [part for parts in groups for part in parts]
        self.specs = [ANY_SPEC] * len(self.args)
        dims = [
            tuple(i.stop - i.start for i in index if isinstance(i, slice))
            + array.shape[len(index) :]
            for array, index in pairs
        ]
        self.scratch = [
            pltpu.VMEM(size, array.dtype) for size, (array, _) in zip(dims, pairs)
        ] + [pltpu.SemaphoreType.DMA((max(1, len(args)),))]
        if groups:
            self.args.append(which)
            self.specs.append(SMEM_SPEC)
        self.loading = [pltpu.VMEM((self.count,) + parts[0].shape, BF16) for parts in groups]
        if groups:
            self.loading.append(pltpu.SemaphoreType.DMA((len(groups), self.count, CHUNKS)))

    def run(self, args, outs, scratch):
        plain, rest = args[: self.plain], list(args[self.plain :])
        held, sems, loading = scratch[: self.plain], scratch[self.plain], scratch[self.plain + 1 :]
        copies = [
            pltpu.make_async_copy(ref.at[index] if index else ref, copy, sems.at[i])
            for i, (ref, index, copy) in enumerate(zip(plain, self.index, held))
        ]
        for copy in copies:
            copy.start()
        loader = []
        if self.groups:
            groups = [[rest.pop(0) for _ in parts] for parts in self.groups]
            loader = [Loader(rest[0], groups, loading[:-1], loading[-1], self.count)]
        for copy in copies:
            copy.wait()
        return self.body(*loader, *held, *outs)


class Loader:
    def __init__(self, which_ref, groups, buffers, sems, count):
        self.groups, self.buffers, self.sems, self.count = groups, buffers, sems, count
        for i in range(count):
            for chunk in range(CHUNKS):
                for group, parts in enumerate(groups):
                    for k, part in enumerate(parts):
                        pl.when(which_ref[i] == k)(self.copy(part, group, i, chunk).start)

    def copy(self, part, group, i, chunk):
        rows = part.shape[0] // CHUNKS
        at = pl.ds(chunk * rows, rows)
        return pltpu.make_async_copy(
            part.at[at], self.buffers[group].at[i, at], self.sems.at[group, i, chunk]
        )

    def rows(self, group, i, chunk):
        part = self.groups[group][0]
        self.copy(part, group, i, chunk).wait()
        count = part.shape[0] // CHUNKS
        at = slice(chunk * count, (chunk + 1) * count)
        return at, self.buffers[group][i, at]


def call(works, outs, after=(), flag=None):
    works = works if isinstance(works, list) else [works]
    flags = [] if flag is None else [flag.reshape(1)]
    sizes = [len(work.args) if work else 0 for work in works]
    loads = [work.loading for work in works if work and work.loading]
    scratch = [item for work in works if work for item in work.scratch] + (loads or [[]])[0]
    extra = len(after) + len(flags)

    def body(*refs):
        refs = list(refs)
        take = lambda n: [refs.pop(0) for _ in range(n)]
        flag_ref = take(len(flags))
        operands = [take(size) for size in sizes]
        take(len(after))
        results = take(len(outs))
        for number, work in enumerate(works):
            if work:
                held = take(len(work.scratch))
                loading = refs[len(refs) - len(work.loading) :]
                run = functools.partial(work.run, operands[number], results, held + loading)
                if flag_ref:
                    pl.when(flag_ref[0][0] == number)(run)
                else:
                    run()

    return pl.pallas_call(
        body,
        in_specs=[SMEM_SPEC] * len(flags)
        + [spec for work in works if work for spec in work.specs]
        + [ANY_SPEC] * len(after),
        out_specs=[VMEM_SPEC] * len(outs),
        out_shape=list(outs),
        scratch_shapes=scratch,
        compiler_params=pltpu.CompilerParams(vmem_limit_bytes=VMEM),
        cost_estimate=pl.CostEstimate(flops=1024, bytes_accessed=1024, transcendentals=0),
    )(*flags, *[arg for work in works if work for arg in work.args], *after)


def tie(value, *after):
    def body(*refs):
        pass

    return pl.pallas_call(
        body,
        in_specs=[ANY_SPEC] * (1 + len(after)),
        out_specs=ANY_SPEC,
        out_shape=jax.ShapeDtypeStruct(value.shape, value.dtype),
        input_output_aliases={0: 0},
        cost_estimate=pl.CostEstimate(flops=0, bytes_accessed=0, transcendentals=0),
    )(value, *after)


def summed(loader, blocks, start=None):
    totals = []
    for group in range(len(loader.groups)):
        total = start
        for i, block in enumerate(blocks):
            for chunk in range(CHUNKS):
                at, rows = loader.rows(group, i, chunk)
                term = dot(block[:, at], rows)
                total = term if total is None else total + term
        totals.append(total)
    return totals[0] if len(totals) == 1 else jnp.concatenate(totals, 1)


def inverse_of(squares):
    return lax.rsqrt(squares / MODEL_WIDTH + NORM_EPS)


def sum_body(count, loader, *refs):
    blocks = [ref[...] for ref in refs[:count]]
    refs[-1][...] = summed(loader, blocks, refs[count][...] if len(refs) > count + 1 else None)


def last_sum_body(loader, first_ref, second_ref, before_ref, squares_ref, *outs):
    total = summed(loader, [first_ref[...], second_ref[...]], before_ref[...])
    rows = (total * inverse_of(squares_ref[...])).astype(BF16)
    length = outs[0].shape[0]
    for i, out in enumerate(outs):
        out[...] = rows[i * length : (i + 1) * length]


def stacked(value, first, per_key):
    return jnp.concatenate(
        [value[:, (first + a) * HEAD_SIZE : (first + a + 1) * HEAD_SIZE] for a in range(per_key)], 0
    )


def allowed_pairs(docs_ref, per_key):
    length = docs_ref.shape[1]
    docs = jnp.broadcast_to(docs_ref[...].astype(F32), (length, length))
    down = lax.broadcasted_iota(jnp.int32, (length, length), 0)
    across = lax.broadcasted_iota(jnp.int32, (length, length), 1)
    allowed = jnp.where(jnp.logical_and(docs.T == docs, down >= across), 1.0, 0.0)
    return jnp.concatenate([allowed] * per_key, 0) > 0.5


def masked_probs(rows, keys, allowed):
    scores = dot(rows, keys, NEAR) * HEAD_SIZE ** (-0.5)
    raised = jnp.where(allowed, jnp.exp(scores), 0.0)
    return raised / jnp.sum(raised, axis=-1, keepdims=True)


def mix(kv_heads, rows, docs_ref):
    length = rows.shape[0]
    query_cols = rows.shape[1] - 2 * kv_heads * HEAD_SIZE
    per_key = query_cols // (kv_heads * HEAD_SIZE)
    allowed = allowed_pairs(docs_ref, per_key)
    out = []
    for head in range(kv_heads):
        key_at = query_cols + head * HEAD_SIZE
        value_at = key_at + kv_heads * HEAD_SIZE
        query = stacked(rows, head * per_key, per_key)
        probs = masked_probs(query, rows[:, key_at : key_at + HEAD_SIZE], allowed)
        mixed = dot(probs.astype(BF16), rows[:, value_at : value_at + HEAD_SIZE]).astype(BF16)
        out += [mixed[a * length : (a + 1) * length] for a in range(per_key)]
    return jnp.concatenate(out, 1)


def two_lanes(value):
    high = value.astype(BF16).astype(F32)
    lane = lax.broadcasted_iota(jnp.int32, (value.shape[0], HEAD_SIZE), 1)
    return jnp.where(lane == 0, high, jnp.where(lane == 1, value - high, 0.0)).astype(BF16)


def head_grads(kv_heads, rows, docs_ref, terms):
    length = rows.shape[0]
    query_cols = rows.shape[1] - 2 * kv_heads * HEAD_SIZE
    per_key = query_cols // (kv_heads * HEAD_SIZE)
    allowed = allowed_pairs(docs_ref, per_key)
    total = terms[0][...].astype(F32)
    for term in terms[1:]:
        total = total + term[...].astype(F32)
    grads = total.astype(BF16)
    row_dot = jnp.zeros((length, 1), F32)
    query_grads, key_grads, value_grads = [], [], []
    for head in range(kv_heads):
        key_at = query_cols + head * HEAD_SIZE
        value_at = key_at + kv_heads * HEAD_SIZE
        query = stacked(rows, head * per_key, per_key)
        keys = rows[:, key_at : key_at + HEAD_SIZE]
        values = rows[:, value_at : value_at + HEAD_SIZE]
        probs = masked_probs(query, keys, allowed)
        grad = stacked(grads, head * per_key, per_key)
        prob_grad = dot(grad, values, NEAR)
        inner = jnp.sum(probs * prob_grad, axis=-1, keepdims=True)
        score_grad = (probs * (prob_grad - inner) * HEAD_SIZE ** (-0.5)).astype(BF16)
        query_grad = dot(score_grad, keys)
        key_grad = dot(score_grad, query, FIRST)
        value_grad = dot(probs.astype(BF16), grad, FIRST)
        products = jnp.sum(query_grad * query.astype(F32), axis=-1, keepdims=True)
        for a in range(per_key):
            at = slice(a * length, (a + 1) * length)
            query_grads.append(query_grad[at].astype(BF16))
            row_dot = row_dot + products[at]
        row_dot = row_dot + jnp.sum(key_grad * keys.astype(F32), axis=-1, keepdims=True)
        row_dot = row_dot + jnp.sum(value_grad * values.astype(F32), axis=-1, keepdims=True)
        key_grads.append(key_grad)
        value_grads.append(value_grad)
    return query_grads, key_grads + value_grads, two_lanes(row_dot)


def turned(loader, lefts, outs):
    for i, out in enumerate(outs):
        for chunk in range(CHUNKS):
            total = 0.0
            for group, left in enumerate(lefts):
                at, rows = loader.rows(group, i, chunk)
                total = total + dot(left, rows, NEAR)
            out[: total.shape[0], at] = total.astype(BF16)


def spread(block, outs):
    for out in outs:
        out[: block.shape[0], : block.shape[1]] = block


def spread_body(block_ref, *outs):
    spread(block_ref[...], outs)


def spread_two_body(first_ref, second_ref, *outs):
    spread(first_ref[...], outs[: len(outs) // 2])
    spread(second_ref[...], outs[len(outs) // 2 :])


def turned_two_body(loader, first_ref, second_ref, *outs):
    length = first_ref.shape[0]
    left = jnp.concatenate([first_ref[...], second_ref[...]], 0)
    for i in range(loader.count):
        for chunk in range(CHUNKS):
            at, rows = loader.rows(0, i, chunk)
            total = dot(left, rows, NEAR).astype(BF16)
            outs[i][:, at] = total[:length]
            outs[loader.count + i][:, at] = total[length:]


def turned_body(count, loader, *refs):
    turned(loader, [ref[...] for ref in refs[:count]], refs[count:])


def mix_body(kv_heads, rows_ref, docs_ref, *outs):
    spread(mix(kv_heads, rows_ref[...], docs_ref), outs)


def project_mix_body(kv_heads, loader, *refs):
    count = loader.count
    blocks, gains = refs[:count], refs[count : 2 * count]
    docs_ref, outs = refs[2 * count], refs[2 * count + 1 :]
    width = gains[0].shape[1]
    squares, scaled = 0.0, []
    for block, gain in zip(blocks, gains):
        block = block[:, :width].astype(F32)
        squares = squares + jnp.sum(block * block, axis=-1, keepdims=True)
        scaled.append((block * gain[...]).astype(BF16))
    rows = (summed(loader, scaled) * inverse_of(squares)).astype(BF16)
    spread(mix(kv_heads, rows, docs_ref), outs)


def back_body(kv_heads, count, loader, rows_ref, docs_ref, *refs):
    length = rows_ref.shape[0]
    terms, outs = refs[:count], refs[-loader.count :]
    query_grads, kv_grads, lanes = head_grads(kv_heads, rows_ref[...], docs_ref, terms)
    left = jnp.concatenate(query_grads + [grad.astype(BF16) for grad in kv_grads], 1)
    turned(loader, [left], outs)
    for i, out in enumerate(outs):
        out[:length, -HEAD_SIZE:] = lanes
        if out.shape[0] > length:
            share = refs[count][i : i + 1]
            high = share.astype(BF16).astype(F32)
            middle = (share - high).astype(BF16).astype(F32)
            row = lax.broadcasted_iota(jnp.int32, (out.shape[0] - length, share.shape[1]), 0)
            low = jnp.where(row == 2, share - high - middle, 0.0)
            out[length:, : share.shape[1]] = jnp.where(
                row == 0, high, jnp.where(row == 1, middle, low)
            ).astype(BF16)


def gain_body(kv_heads, count, loader, rows_ref, docs_ref, squares_ref, hidden_ref, *refs):
    terms, out = refs[:count], refs[count]
    query_grads, kv_grads, _ = head_grads(kv_heads, rows_ref[...], docs_ref, terms)
    left = jnp.concatenate(query_grads + [grad.astype(BF16) for grad in kv_grads], 1)
    inverse = inverse_of(squares_ref[...])
    for i in range(loader.count):
        for chunk in range(CHUNKS):
            at, rows = loader.rows(0, i, chunk)
            term = dot(left, rows, NEAR) * (hidden_ref[i, :, at].astype(F32) * inverse)
            out[i : i + 1, at] = jnp.sum(term, axis=0, keepdims=True)


def heads_body(kv_heads, count, rows_ref, docs_ref, *refs):
    terms, (query_ref, kv_ref, lanes_ref) = refs[:count], refs[count:]
    query_grads, kv_grads, lanes = head_grads(kv_heads, rows_ref[...], docs_ref, terms)
    query_ref[...] = jnp.concatenate(query_grads, 1)
    kv_ref[...] = jnp.concatenate(kv_grads, 1).astype(kv_ref.dtype)
    lanes_ref[...] = lanes


def out_body(loader, hidden_ref, *refs):
    blocks, outs = refs[: loader.count], refs[loader.count :]
    length, width = hidden_ref.shape[0], loader.groups[0][0].shape[0]
    total = summed(loader, [block[:length, :width] for block in blocks])
    outs[0][...] = (hidden_ref[...].astype(F32) + total).astype(BF16)
    for out in outs[1:]:
        out[...] = jnp.zeros_like(out)


def result_body(count, hidden_ref, grad_ref, gain_ref, squares_ref, *refs):
    terms, sides, (result_ref, term_ref) = refs[:count], refs[count:-2], refs[-2:]
    length, width = hidden_ref.shape
    normed_grad = sum(term[:length, :width].astype(F32) for term in terms)
    lanes = sum(side[:length, -HEAD_SIZE:].astype(F32) for side in sides or terms)
    inverse = inverse_of(squares_ref[...])
    row_dot = (lanes[:, :1] + lanes[:, 1:2]) / inverse
    hidden = hidden_ref[...].astype(F32)
    result_ref[...] = (
        grad_ref[...].astype(F32)
        + inverse * (normed_grad * gain_ref[...])
        - hidden * (inverse * inverse * inverse * row_dot / MODEL_WIDTH)
    ).astype(BF16)
    total = jnp.sum(normed_grad * hidden * inverse, axis=0, keepdims=True)
    if terms[0].shape[0] > length:
        total = total + sum(
            jnp.sum(term[length:, :width].astype(F32), axis=0, keepdims=True) for term in terms
        )
    term_ref[...] = total


def split_float(value):
    high = lax.reduce_precision(value, 8, 7)
    middle = lax.reduce_precision(value - high, 8, 7)
    return [high.astype(BF16), middle.astype(BF16), (value - high - middle).astype(BF16)]


def local(
    arrivals,
    fresh,
    stash,
    returning,
    loss_grad,
    gain,
    query_weight,
    key_weight,
    value_weight,
    w_out,
    plan,
    fresh_docs,
    arrival_docs,
    stash_docs,
):
    tensor_count = lax.axis_size("tensor")
    section_count = lax.axis_size("section")
    replicas = lax.axis_size("dp")
    tensor_pos = lax.axis_index("tensor")
    section_pos = lax.axis_index("section")
    replica_pos = lax.axis_index("dp")
    length, width = arrivals.shape[2:]
    heads_here = QUERY_HEADS // tensor_count
    group_width = QUERY_HEADS // KEY_VALUE_HEADS
    share_count = max(1, group_width // heads_here)
    bit_count = share_count.bit_length() - 1
    query_cols = heads_here * HEAD_SIZE
    block_rows = query_weight.shape[1]
    every = range(section_count)
    paired = tensor_count == replicas and section_count == 2
    shift = tensor_pos if paired else 0
    first = (section_pos == 0).astype(jnp.int32)
    last = (section_pos == section_count - 1).astype(jnp.int32)
    which = [(replica_pos ^ mask ^ shift).astype(jnp.int32) for mask in range(replicas)]
    picks = jnp.stack(which)

    def fixed(*masks):
        return jnp.array(masks, jnp.int32)

    def gather_dp(weight):
        other = exchange(weight, "dp", 2)
        return [weight, exchange(weight, "dp", 1), other, exchange(other, "dp", 1)]

    def gather(block):
        whole = lax.all_gather(block, "tensor", axis=1, tiled=True)
        return jnp.split(whole, replicas, 1)

    def swap(blocks, sections=every):
        far, middle, near = [exchange_tensor(blocks[mask], mask, sections) for mask in (3, 2, 1)]
        return [blocks[0], near, middle, far]

    def whole_scatter(lefts, groups, aside=None):
        part = call(
            Work(functools.partial(turned_body, len(lefts)), lefts, groups, picks),
            [shape(length, block_rows, BF16)] * replicas,
        )
        part = jnp.concatenate(part, 1)
        terms = [lax.psum_scatter(part, "tensor", scatter_dimension=1, tiled=True)]
        if aside is None:
            return terms, []
        total = lax.psum(aside[:, :2].astype(F32), "tensor")
        rest = jnp.zeros((length, HEAD_SIZE - 2), F32)
        return terms, [jnp.concatenate([total, rest], 1)]

    def balance(rows, *after):
        sibling = exchange(rows, "dp", 1)
        asked = plan[:, replica_pos ^ 2][:, None, None]
        source = plan[:, replica_pos][:, None, None]
        far = exchange(tie(jnp.where(asked == replica_pos, rows, sibling), *after), "dp", 2)
        return jnp.where(
            source == replica_pos, rows, jnp.where(source == replica_pos ^ 1, sibling, far)
        )

    def forward_documents(tick):
        from_arrivals = lax.dynamic_index_in_dim(
            arrival_docs, jnp.clip(section_pos - tick - 1, 0, section_count - 1), 0, keepdims=False
        )[0]
        step = jnp.clip(tick - section_pos, 0, TICKS - 1)
        from_fresh = fresh_docs[step, plan[step, replica_pos]]
        return jnp.where(section_pos > tick, from_arrivals, from_fresh)[None, :]

    own_kv = [key_weight[0], value_weight[0]]
    pair_kv = own_kv
    for bit in range(bit_count):
        low_side = tensor_pos >> bit & 1 == 0
        partners = [exchange(block, "tensor", 1 << bit) for block in pair_kv]
        pair_kv = [
            jnp.where(
                low_side,
                jnp.concatenate([block, partner], -1),
                jnp.concatenate([partner, block], -1),
            )
            for block, partner in zip(pair_kv, partners)
        ]
    head_cols = pair_kv[0].shape[1]
    kv_heads = head_cols // HEAD_SIZE
    own_weight = jnp.concatenate([query_weight[0], *pair_kv], 1)
    out_x, weight_x = [exchange(weight, "dp", 2) for weight in (w_out[0], own_weight)]
    out_sibling, weight_sibling = [exchange(weight, "dp", 1) for weight in (w_out[0], own_weight)]
    grad_in = jnp.where(
        section_pos == section_count - 1,
        loss_grad[0, 0],
        shifted(returning[0, 0], "section", -1),
    )
    new_docs = [forward_documents(tick) for tick in range(TICKS)]
    old_docs = [stash_docs[tick, 0, 0][None, :] for tick in range(TICKS)]
    balanced = balance(fresh[:, 0], own_weight, grad_in, *new_docs, *old_docs)
    out_x = tie(out_x, balanced)
    out_parts = [w_out[0], out_sibling, out_x, exchange(out_x, "dp", 1)]

    first_in = balanced[0]
    if section_count > TICKS:
        first_in = jnp.where(section_pos == 0, first_in, shifted(arrivals[0, 0], "section", 1))
    gain_rows = jnp.stack(split_float(gain[0]) + [jnp.zeros((width,), BF16)] * 13)
    early = jnp.concatenate([stash[0, 0, 0], stash[1, 0, 0], gain_rows], 0)
    early = lax.all_gather(early, "tensor")

    def early_block(index):
        group = tensor_count // replicas
        block = lax.dynamic_slice_in_dim(early, index * group, group, 0)
        return block.transpose(1, 0, 2).reshape(early.shape[1], block_rows)

    def gain_of(block):
        return sum(block[-16 + i : -15 + i].astype(F32) for i in range(3))

    narrow = [shape(length, block_rows, BF16)] * replicas
    if paired:
        sent = call(
            [
                Work(spread_two_body, [(balanced, (0,)), (balanced, (1,))]),
                Work(
                    turned_two_body, [(loss_grad, (0, 0)), (loss_grad, (1, 0))], [out_parts], picks
                ),
            ],
            narrow * 2,
            (),
            last,
        )
        firsts = swap(sent[:replicas])
        seconds = swap(sent[replicas:])
        sent = call(
            [Work(functools.partial(turned_body, 1), [grad_in], [out_parts], picks), None],
            narrow,
            firsts[1:3],
            last,
        )
        heads = swap(sent, every[:1])
    else:
        firsts = gather(first_in)
        heads, _ = whole_scatter([grad_in], [out_parts])
    mine = jnp.stack(firsts)

    saved = TICKS * length
    squares = jnp.sum(jnp.square(early[:, :saved].astype(F32)), (0, 2))
    blocks = [early_block(replica_pos ^ mask) for mask in range(replicas)]
    turns = [gain_of(block) for block in blocks]
    rows = [
        (block[:saved].astype(F32) * gain_block).astype(BF16)
        for block, gain_block in zip(blocks, turns)
    ]
    squares = jnp.concatenate([squares, jnp.sum(jnp.square(mine.astype(F32)), (0, 2))])[:, None]
    for mask in range(replicas):
        block = lax.dynamic_index_in_dim(mine, which[mask], 0, keepdims=False).astype(F32)
        rows[mask] = jnp.concatenate([rows[mask], (block * turns[mask]).astype(BF16)], 0)
    gains = [gain_of(early_block(mask ^ shift)) for mask in range(replicas)]
    (total,) = call(
        Work(
            functools.partial(sum_body, 2), rows[:2], [[own_weight, weight_sibling]], fixed(0, 1)
        ),
        [shape(saved + length, own_weight.shape[1])],
        seconds[1:] if paired else (),
    )
    weight_x = tie(weight_x, total, rows[2], rows[3], squares, *heads[1:])
    parts = [own_weight, weight_sibling, weight_x, exchange(weight_x, "dp", 1)]
    states = call(
        Work(last_sum_body, [rows[2], rows[3], total, squares], [parts[2:]], fixed(0, 1)),
        [shape(length, own_weight.shape[1], BF16)] * 3,
    )
    old_squares = [squares[tick * length : (tick + 1) * length] for tick in range(TICKS)]
    wide = [shape(length, block_rows + HEAD_SIZE, BF16)] * replicas
    sent_type = [shape(length, width, BF16), shape(1, width)]

    def mix_work(state, documents):
        return Work(functools.partial(mix_body, kv_heads), [state, documents])

    def project_mix_work(blocks):
        return Work(
            functools.partial(project_mix_body, kv_heads),
            [*blocks, *gains, new_docs[1]],
            [parts],
            picks,
        )

    def back_work(state, documents, terms, *shares):
        return Work(
            functools.partial(back_body, kv_heads, len(terms)),
            [state, documents, *terms, *shares],
            [parts],
            picks,
        )

    def out_work(hidden, blocks):
        return Work(out_body, [hidden, *blocks], [out_parts], picks)

    def result_work(tick, grad, terms, sides=()):
        return Work(
            functools.partial(result_body, len(terms)),
            [(stash, (tick, 0, 0)), grad, gain, old_squares[tick], *terms, *sides],
        )

    if paired:
        swapped = swap(
            call(
                [mix_work(states[2], new_docs[0]), back_work(states[0], old_docs[0], firsts)],
                wide,
                (),
                last,
            )
        )
        apart_sent = call(
            [project_mix_work(seconds), back_work(states[1], old_docs[1], seconds)],
            wide,
            swapped[1:2],
            last,
        )
        apart = swap(apart_sent)
        sent, gain_0 = call(
            [out_work((balanced, (0,)), swapped), result_work(0, (loss_grad, (0, 0)), swapped)],
            sent_type,
            apart_sent[:1],
            last,
        )
        arrived = exchange(sent, "section", 1)
        swapped = swap(
            call(
                [
                    Work(functools.partial(turned_body, 1), [arrived], [out_parts], picks),
                    Work(spread_body, [arrived]),
                ],
                narrow,
                apart[1:],
                last,
            )
        )
        saved_blocks = jnp.stack([early_block(tensor_pos ^ mask)[:length] for mask in range(replicas)])
        (shares,) = call(
            [
                Work(
                    functools.partial(gain_body, kv_heads, replicas),
                    [states[0], old_docs[0], old_squares[0], saved_blocks, *heads],
                    [parts],
                    picks,
                ),
                Work(lambda ref: spread(jnp.zeros_like(ref), [ref]), []),
            ],
            [shape(replicas, block_rows)],
            swapped[1:2],
            last,
        )
        swapped = swap(
            call(
                [back_work(states[1], old_docs[1], swapped, shares), project_mix_work(swapped)],
                [shape(length + 16, block_rows + HEAD_SIZE, BF16)] * replicas,
                (),
                last,
            )
        )
        early_out, gain_1 = call(
            [out_work((balanced, (1,)), apart), result_work(1, (loss_grad, (1, 0)), apart)],
            sent_type,
            swapped[1:2],
            last,
        )
        late_out, gain_3 = call(
            [result_work(1, arrived, swapped), out_work(arrived, swapped)],
            sent_type,
            [early_out],
            last,
        )
        outgoing = jnp.where(last == 1, late_out, early_out)
        going_back = jnp.where(last == 1, early_out, late_out)
        gain_total = gain_0 + gain_1 + gain_3
    else:
        grad_groups = [parts]
        if bit_count:
            grad_groups = [gather_dp(query_weight[0]), gather_dp(jnp.concatenate(own_kv, 1))]
        gain_total = jnp.zeros((1, width), F32)
        hidden = first_in
        for tick in range(TICKS):
            if tick:
                hidden = jnp.where(first == 1, balanced[1], shifted(outgoing, "section", 1))
                grad_in = jnp.where(
                    last == 1, loss_grad[1, 0], shifted(going_back, "section", -1)
                )
                mixed_work = project_mix_work(gather(hidden))
                heads, _ = whole_scatter([grad_in], [out_parts])
            else:
                mixed_work = mix_work(states[2], new_docs[0])
            (mixed,) = call(mixed_work, [shape(length, query_cols, BF16)])
            (outgoing,) = call(out_work(hidden, gather(mixed)), sent_type[:1])
            query_grad, kv_grad, aside = call(
                Work(
                    functools.partial(heads_body, kv_heads, len(heads)),
                    [states[tick], old_docs[tick], *heads],
                ),
                [
                    shape(length, query_cols, BF16),
                    shape(length, 2 * head_cols, F32 if bit_count else BF16),
                    shape(length, HEAD_SIZE, BF16),
                ],
            )
            grads = [jnp.concatenate([query_grad, kv_grad.astype(BF16)], 1)]
            if bit_count:
                kv_grad = jnp.stack([kv_grad[:, :head_cols], kv_grad[:, head_cols:]])
                for bit in reversed(range(bit_count)):
                    half = kv_grad.shape[-1] // 2
                    low_side = tensor_pos >> bit & 1 == 0
                    keep = jnp.where(low_side, kv_grad[..., :half], kv_grad[..., half:])
                    outward = jnp.where(low_side, kv_grad[..., half:], kv_grad[..., :half])
                    kv_grad = keep + exchange(outward.astype(BF16), "tensor", 1 << bit).astype(F32)
                grads = [query_grad, jnp.concatenate([kv_grad[0], kv_grad[1]], 1).astype(BF16)]
            terms, sides = whole_scatter(grads, grad_groups, aside)
            going_back, gain_term = call(result_work(tick, grad_in, terms, sides), sent_type)
            gain_total = gain_total + gain_term
    gain_total = gain_total + exchange(gain_total, "dp", 1)
    gain_total = gain_total + exchange(gain_total, "dp", 2)
    gain_grad = gain_total / math.sqrt(TICKS * replicas * length)
    return (outgoing[None, None], going_back[None, None], gain_grad)


def solution(mesh):
    return jax.shard_map(
        local,
        mesh=mesh,
        in_specs=(
            P("section", "dp", None, "tensor"),
            P(None, "dp", None, "tensor"),
            P(None, "section", "dp", None, "tensor"),
            P("section", "dp", None, "tensor"),
            P(None, "dp", None, "tensor"),
            P("section", "tensor"),
            P("section", "dp", "tensor"),
            P("section", "dp", "tensor"),
            P("section", "dp", "tensor"),
            P("section", "dp", "tensor"),
            P(),
            P(),
            P(None, "dp", None),
            P(None, "section", "dp", None),
        ),
        out_specs=(
            P("section", "dp", None, "tensor"),
            P("section", "dp", None, "tensor"),
            P("section", "tensor"),
        ),
        check_vma=False,
    )
```

```python
import functools
import math

import jax
import jax.numpy as jnp
from jax import lax
from jax.experimental import pallas as pl
from jax.experimental.pallas import tpu as pltpu
from jax.sharding import PartitionSpec as P

MODEL_WIDTH = 4096
QUERY_HEADS = 32
KEY_VALUE_HEADS = 8
HEAD_SIZE = 128
TICKS = 2
NORM_EPS = 1e-05
F32 = jnp.float32
BF16 = jnp.bfloat16


NEAR = (((1,), (1,)), ((), ()))
FIRST = (((0,), (0,)), ((), ()))
CHUNKS = 2
VMEM = 22 * 2**20
SMEM_SPEC = pl.BlockSpec(memory_space=pltpu.SMEM)
ANY_SPEC = pl.BlockSpec(memory_space=pl.ANY)
VMEM_SPEC = pl.BlockSpec(memory_space=pltpu.VMEM)


def exchange(block, axis, mask):
    count = lax.axis_size(axis)
    return lax.ppermute(block, axis, [(i, i ^ mask) for i in range(count)])


def exchange_tensor(block, mask, sections):
    count = lax.axis_size("tensor")
    return lax.ppermute(
        block,
        ("section", "tensor"),
        [(s * count + i, s * count + (i ^ mask)) for s in sections for i in range(count)],
    )


def shifted(value, axis, steps):
    count = lax.axis_size(axis)
    leading, last = (max(0, -steps), min(count, count - steps))
    return lax.ppermute(value, axis, [(source, source + steps) for source in range(leading, last)])


def dot(left, right, contract=(((1,), (0,)), ((), ()))):
    return lax.dot_general(left, right, contract, preferred_element_type=F32)


def shape(rows, cols, dtype=F32):
    return jax.ShapeDtypeStruct((rows, cols), dtype)


class Work:
    def __init__(self, body, args, groups=(), which=None):
        self.body, self.groups = body, groups
        self.count = 0 if which is None else which.shape[0]
        pairs = [arg if isinstance(arg, tuple) else (arg, ()) for arg in args]
        self.index = [index for _, index in pairs]
        self.plain = len(args)
        self.args = [array for array, _ in pairs] + [part for parts in groups for part in parts]
        self.specs = [ANY_SPEC] * len(self.args)
        dims = [
            tuple(i.stop - i.start for i in index if isinstance(i, slice))
            + array.shape[len(index) :]
            for array, index in pairs
        ]
        self.scratch = [
            pltpu.VMEM(size, array.dtype) for size, (array, _) in zip(dims, pairs)
        ] + [pltpu.SemaphoreType.DMA((max(1, len(args)),))]
        if groups:
            self.args.append(which)
            self.specs.append(SMEM_SPEC)
        self.loading = [pltpu.VMEM((self.count,) + parts[0].shape, BF16) for parts in groups]
        if groups:
            self.loading.append(pltpu.SemaphoreType.DMA((len(groups), self.count, CHUNKS)))

    def run(self, args, outs, scratch):
        plain, rest = args[: self.plain], list(args[self.plain :])
        held, sems, loading = scratch[: self.plain], scratch[self.plain], scratch[self.plain + 1 :]
        copies = [
            pltpu.make_async_copy(ref.at[index] if index else ref, copy, sems.at[i])
            for i, (ref, index, copy) in enumerate(zip(plain, self.index, held))
        ]
        for copy in copies:
            copy.start()
        loader = []
        if self.groups:
            groups = [[rest.pop(0) for _ in parts] for parts in self.groups]
            loader = [Loader(rest[0], groups, loading[:-1], loading[-1], self.count)]
        for copy in copies:
            copy.wait()
        return self.body(*loader, *held, *outs)


class Loader:
    def __init__(self, which_ref, groups, buffers, sems, count):
        self.groups, self.buffers, self.sems, self.count = groups, buffers, sems, count
        for i in range(count):
            for chunk in range(CHUNKS):
                for group, parts in enumerate(groups):
                    for k, part in enumerate(parts):
                        pl.when(which_ref[i] == k)(self.copy(part, group, i, chunk).start)

    def copy(self, part, group, i, chunk):
        rows = part.shape[0] // CHUNKS
        at = pl.ds(chunk * rows, rows)
        return pltpu.make_async_copy(
            part.at[at], self.buffers[group].at[i, at], self.sems.at[group, i, chunk]
        )

    def rows(self, group, i, chunk):
        part = self.groups[group][0]
        self.copy(part, group, i, chunk).wait()
        count = part.shape[0] // CHUNKS
        at = slice(chunk * count, (chunk + 1) * count)
        return at, self.buffers[group][i, at]


def call(works, outs, after=(), flag=None):
    works = works if isinstance(works, list) else [works]
    flags = [] if flag is None else [flag.reshape(1)]
    sizes = [len(work.args) if work else 0 for work in works]
    loads = [work.loading for work in works if work and work.loading]
    scratch = [item for work in works if work for item in work.scratch] + (loads or [[]])[0]
    extra = len(after) + len(flags)

    def body(*refs):
        refs = list(refs)
        take = lambda n: [refs.pop(0) for _ in range(n)]
        flag_ref = take(len(flags))
        operands = [take(size) for size in sizes]
        take(len(after))
        results = take(len(outs))
        for number, work in enumerate(works):
            if work:
                held = take(len(work.scratch))
                loading = refs[len(refs) - len(work.loading) :]
                run = functools.partial(work.run, operands[number], results, held + loading)
                if flag_ref:
                    pl.when(flag_ref[0][0] == number)(run)
                else:
                    run()

    return pl.pallas_call(
        body,
        in_specs=[SMEM_SPEC] * len(flags)
        + [spec for work in works if work for spec in work.specs]
        + [ANY_SPEC] * len(after),
        out_specs=[VMEM_SPEC] * len(outs),
        out_shape=list(outs),
        scratch_shapes=scratch,
        compiler_params=pltpu.CompilerParams(vmem_limit_bytes=VMEM),
        cost_estimate=pl.CostEstimate(flops=1024, bytes_accessed=1024, transcendentals=0),
    )(*flags, *[arg for work in works if work for arg in work.args], *after)


def tie(value, *after):
    def body(*refs):
        pass

    return pl.pallas_call(
        body,
        in_specs=[ANY_SPEC] * (1 + len(after)),
        out_specs=ANY_SPEC,
        out_shape=jax.ShapeDtypeStruct(value.shape, value.dtype),
        input_output_aliases={0: 0},
        cost_estimate=pl.CostEstimate(flops=0, bytes_accessed=0, transcendentals=0),
    )(value, *after)


def summed(loader, blocks, start=None):
    totals = []
    for group in range(len(loader.groups)):
        total = start
        for i, block in enumerate(blocks):
            for chunk in range(CHUNKS):
                at, rows = loader.rows(group, i, chunk)
                term = dot(block[:, at], rows)
                total = term if total is None else total + term
        totals.append(total)
    return totals[0] if len(totals) == 1 else jnp.concatenate(totals, 1)


def inverse_of(squares):
    return lax.rsqrt(squares / MODEL_WIDTH + NORM_EPS)


def sum_body(count, loader, *refs):
    blocks = [ref[...] for ref in refs[:count]]
    refs[-1][...] = summed(loader, blocks, refs[count][...] if len(refs) > count + 1 else None)


def last_sum_body(loader, first_ref, second_ref, before_ref, squares_ref, *outs):
    total = summed(loader, [first_ref[...], second_ref[...]], before_ref[...])
    rows = (total * inverse_of(squares_ref[...])).astype(BF16)
    length = outs[0].shape[0]
    for i, out in enumerate(outs):
        out[...] = rows[i * length : (i + 1) * length]


def stacked(value, first, per_key):
    return jnp.concatenate(
        [value[:, (first + a) * HEAD_SIZE : (first + a + 1) * HEAD_SIZE] for a in range(per_key)], 0
    )


def allowed_pairs(docs_ref, per_key):
    length = docs_ref.shape[1]
    docs = jnp.broadcast_to(docs_ref[...].astype(F32), (length, length))
    down = lax.broadcasted_iota(jnp.int32, (length, length), 0)
    across = lax.broadcasted_iota(jnp.int32, (length, length), 1)
    allowed = jnp.where(jnp.logical_and(docs.T == docs, down >= across), 1.0, 0.0)
    return jnp.concatenate([allowed] * per_key, 0) > 0.5


def masked_probs(rows, keys, allowed):
    scores = dot(rows, keys, NEAR) * HEAD_SIZE ** (-0.5)
    raised = jnp.where(allowed, jnp.exp(scores), 0.0)
    return raised / jnp.sum(raised, axis=-1, keepdims=True)


def mix(kv_heads, rows, docs_ref):
    length = rows.shape[0]
    query_cols = rows.shape[1] - 2 * kv_heads * HEAD_SIZE
    per_key = query_cols // (kv_heads * HEAD_SIZE)
    allowed = allowed_pairs(docs_ref, per_key)
    out = []
    for head in range(kv_heads):
        key_at = query_cols + head * HEAD_SIZE
        value_at = key_at + kv_heads * HEAD_SIZE
        query = stacked(rows, head * per_key, per_key)
        probs = masked_probs(query, rows[:, key_at : key_at + HEAD_SIZE], allowed)
        mixed = dot(probs.astype(BF16), rows[:, value_at : value_at + HEAD_SIZE]).astype(BF16)
        out += [mixed[a * length : (a + 1) * length] for a in range(per_key)]
    return jnp.concatenate(out, 1)


def two_lanes(value):
    high = value.astype(BF16).astype(F32)
    lane = lax.broadcasted_iota(jnp.int32, (value.shape[0], HEAD_SIZE), 1)
    return jnp.where(lane == 0, high, jnp.where(lane == 1, value - high, 0.0)).astype(BF16)


def head_grads(kv_heads, rows, docs_ref, terms):
    length = rows.shape[0]
    query_cols = rows.shape[1] - 2 * kv_heads * HEAD_SIZE
    per_key = query_cols // (kv_heads * HEAD_SIZE)
    allowed = allowed_pairs(docs_ref, per_key)
    total = terms[0][...].astype(F32)
    for term in terms[1:]:
        total = total + term[...].astype(F32)
    grads = total.astype(BF16)
    row_dot = jnp.zeros((length, 1), F32)
    query_grads, key_grads, value_grads = [], [], []
    for head in range(kv_heads):
        key_at = query_cols + head * HEAD_SIZE
        value_at = key_at + kv_heads * HEAD_SIZE
        query = stacked(rows, head * per_key, per_key)
        keys = rows[:, key_at : key_at + HEAD_SIZE]
        values = rows[:, value_at : value_at + HEAD_SIZE]
        probs = masked_probs(query, keys, allowed)
        grad = stacked(grads, head * per_key, per_key)
        prob_grad = dot(grad, values, NEAR)
        inner = jnp.sum(probs * prob_grad, axis=-1, keepdims=True)
        score_grad = (probs * (prob_grad - inner) * HEAD_SIZE ** (-0.5)).astype(BF16)
        query_grad = dot(score_grad, keys)
        key_grad = dot(score_grad, query, FIRST)
        value_grad = dot(probs.astype(BF16), grad, FIRST)
        products = jnp.sum(query_grad * query.astype(F32), axis=-1, keepdims=True)
        for a in range(per_key):
            at = slice(a * length, (a + 1) * length)
            query_grads.append(query_grad[at].astype(BF16))
            row_dot = row_dot + products[at]
        row_dot = row_dot + jnp.sum(key_grad * keys.astype(F32), axis=-1, keepdims=True)
        row_dot = row_dot + jnp.sum(value_grad * values.astype(F32), axis=-1, keepdims=True)
        key_grads.append(key_grad)
        value_grads.append(value_grad)
    return query_grads, key_grads + value_grads, two_lanes(row_dot)


def turned(loader, lefts, outs):
    for i, out in enumerate(outs):
        for chunk in range(CHUNKS):
            total = 0.0
            for group, left in enumerate(lefts):
                at, rows = loader.rows(group, i, chunk)
                total = total + dot(left, rows, NEAR)
            out[: total.shape[0], at] = total.astype(BF16)


def spread(block, outs):
    for out in outs:
        out[: block.shape[0], : block.shape[1]] = block


def spread_body(block_ref, *outs):
    spread(block_ref[...], outs)


def spread_two_body(first_ref, second_ref, *outs):
    spread(first_ref[...], outs[: len(outs) // 2])
    spread(second_ref[...], outs[len(outs) // 2 :])


def turned_two_body(loader, first_ref, second_ref, *outs):
    length = first_ref.shape[0]
    left = jnp.concatenate([first_ref[...], second_ref[...]], 0)
    for i in range(loader.count):
        for chunk in range(CHUNKS):
            at, rows = loader.rows(0, i, chunk)
            total = dot(left, rows, NEAR).astype(BF16)
            outs[i][:, at] = total[:length]
            outs[loader.count + i][:, at] = total[length:]


def turned_body(count, loader, *refs):
    turned(loader, [ref[...] for ref in refs[:count]], refs[count:])


def mix_body(kv_heads, rows_ref, docs_ref, *outs):
    spread(mix(kv_heads, rows_ref[...], docs_ref), outs)


def project_mix_body(kv_heads, loader, *refs):
    count = loader.count
    blocks, gains = refs[:count], refs[count : 2 * count]
    docs_ref, outs = refs[2 * count], refs[2 * count + 1 :]
    width = gains[0].shape[1]
    squares, scaled = 0.0, []
    for block, gain in zip(blocks, gains):
        block = block[:, :width].astype(F32)
        squares = squares + jnp.sum(block * block, axis=-1, keepdims=True)
        scaled.append((block * gain[...]).astype(BF16))
    rows = (summed(loader, scaled) * inverse_of(squares)).astype(BF16)
    spread(mix(kv_heads, rows, docs_ref), outs)


def back_body(kv_heads, count, loader, rows_ref, docs_ref, *refs):
    length = rows_ref.shape[0]
    terms, outs = refs[:count], refs[-loader.count :]
    query_grads, kv_grads, lanes = head_grads(kv_heads, rows_ref[...], docs_ref, terms)
    left = jnp.concatenate(query_grads + [grad.astype(BF16) for grad in kv_grads], 1)
    turned(loader, [left], outs)
    for i, out in enumerate(outs):
        out[:length, -HEAD_SIZE:] = lanes
        if out.shape[0] > length:
            share = refs[count][i : i + 1]
            high = share.astype(BF16).astype(F32)
            middle = (share - high).astype(BF16).astype(F32)
            row = lax.broadcasted_iota(jnp.int32, (out.shape[0] - length, share.shape[1]), 0)
            low = jnp.where(row == 2, share - high - middle, 0.0)
            out[length:, : share.shape[1]] = jnp.where(
                row == 0, high, jnp.where(row == 1, middle, low)
            ).astype(BF16)


def gain_body(kv_heads, count, loader, rows_ref, docs_ref, squares_ref, hidden_ref, *refs):
    terms, out = refs[:count], refs[count]
    query_grads, kv_grads, _ = head_grads(kv_heads, rows_ref[...], docs_ref, terms)
    left = jnp.concatenate(query_grads + [grad.astype(BF16) for grad in kv_grads], 1)
    inverse = inverse_of(squares_ref[...])
    for i in range(loader.count):
        for chunk in range(CHUNKS):
            at, rows = loader.rows(0, i, chunk)
            term = dot(left, rows, NEAR) * (hidden_ref[i, :, at].astype(F32) * inverse)
            out[i : i + 1, at] = jnp.sum(term, axis=0, keepdims=True)


def heads_body(kv_heads, count, rows_ref, docs_ref, *refs):
    terms, (query_ref, kv_ref, lanes_ref) = refs[:count], refs[count:]
    query_grads, kv_grads, lanes = head_grads(kv_heads, rows_ref[...], docs_ref, terms)
    query_ref[...] = jnp.concatenate(query_grads, 1)
    kv_ref[...] = jnp.concatenate(kv_grads, 1).astype(kv_ref.dtype)
    lanes_ref[...] = lanes


def out_body(loader, hidden_ref, *refs):
    blocks, outs = refs[: loader.count], refs[loader.count :]
    length, width = hidden_ref.shape[0], loader.groups[0][0].shape[0]
    total = summed(loader, [block[:length, :width] for block in blocks])
    outs[0][...] = (hidden_ref[...].astype(F32) + total).astype(BF16)
    for out in outs[1:]:
        out[...] = jnp.zeros_like(out)


def result_body(count, hidden_ref, grad_ref, gain_ref, squares_ref, *refs):
    terms, sides, (result_ref, term_ref) = refs[:count], refs[count:-2], refs[-2:]
    length, width = hidden_ref.shape
    normed_grad = sum(term[:length, :width].astype(F32) for term in terms)
    lanes = sum(side[:length, -HEAD_SIZE:].astype(F32) for side in sides or terms)
    inverse = inverse_of(squares_ref[...])
    row_dot = (lanes[:, :1] + lanes[:, 1:2]) / inverse
    hidden = hidden_ref[...].astype(F32)
    result_ref[...] = (
        grad_ref[...].astype(F32)
        + inverse * (normed_grad * gain_ref[...])
        - hidden * (inverse * inverse * inverse * row_dot / MODEL_WIDTH)
    ).astype(BF16)
    total = jnp.sum(normed_grad * hidden * inverse, axis=0, keepdims=True)
    if terms[0].shape[0] > length:
        total = total + sum(
            jnp.sum(term[length:, :width].astype(F32), axis=0, keepdims=True) for term in terms
        )
    term_ref[...] = total


def split_float(value):
    high = lax.reduce_precision(value, 8, 7)
    middle = lax.reduce_precision(value - high, 8, 7)
    return [high.astype(BF16), middle.astype(BF16), (value - high - middle).astype(BF16)]


def local(
    arrivals,
    fresh,
    stash,
    returning,
    loss_grad,
    gain,
    query_weight,
    key_weight,
    value_weight,
    w_out,
    plan,
    fresh_docs,
    arrival_docs,
    stash_docs,
):
    tensor_count = lax.axis_size("tensor")
    section_count = lax.axis_size("section")
    replicas = lax.axis_size("dp")
    tensor_pos = lax.axis_index("tensor")
    section_pos = lax.axis_index("section")
    replica_pos = lax.axis_index("dp")
    length, width = arrivals.shape[2:]
    heads_here = QUERY_HEADS // tensor_count
    group_width = QUERY_HEADS // KEY_VALUE_HEADS
    share_count = max(1, group_width // heads_here)
    bit_count = share_count.bit_length() - 1
    query_cols = heads_here * HEAD_SIZE
    block_rows = query_weight.shape[1]
    every = range(section_count)
    paired = tensor_count == replicas and section_count == 2
    shift = tensor_pos if paired else 0
    first = (section_pos == 0).astype(jnp.int32)
    last = (section_pos == section_count - 1).astype(jnp.int32)
    which = [(replica_pos ^ mask ^ shift).astype(jnp.int32) for mask in range(replicas)]
    picks = jnp.stack(which)

    def fixed(*masks):
        return jnp.array(masks, jnp.int32)

    def gather_dp(weight):
        other = exchange(weight, "dp", 2)
        return [weight, exchange(weight, "dp", 1), other, exchange(other, "dp", 1)]

    def gather(block):
        whole = lax.all_gather(block, "tensor", axis=1, tiled=True)
        return jnp.split(whole, replicas, 1)

    def swap(blocks, sections=every):
        far, middle, near = [exchange_tensor(blocks[mask], mask, sections) for mask in (3, 2, 1)]
        return [blocks[0], near, middle, far]

    def whole_scatter(lefts, groups, aside=None):
        part = call(
            Work(functools.partial(turned_body, len(lefts)), lefts, groups, picks),
            [shape(length, block_rows, BF16)] * replicas,
        )
        part = jnp.concatenate(part, 1)
        terms = [lax.psum_scatter(part, "tensor", scatter_dimension=1, tiled=True)]
        if aside is None:
            return terms, []
        total = lax.psum(aside[:, :2].astype(F32), "tensor")
        rest = jnp.zeros((length, HEAD_SIZE - 2), F32)
        return terms, [jnp.concatenate([total, rest], 1)]

    def balance(rows, *after):
        sibling = exchange(rows, "dp", 1)
        asked = plan[:, replica_pos ^ 2][:, None, None]
        source = plan[:, replica_pos][:, None, None]
        far = exchange(tie(jnp.where(asked == replica_pos, rows, sibling), *after), "dp", 2)
        return jnp.where(
            source == replica_pos, rows, jnp.where(source == replica_pos ^ 1, sibling, far)
        )

    def forward_documents(tick):
        from_arrivals = lax.dynamic_index_in_dim(
            arrival_docs, jnp.clip(section_pos - tick - 1, 0, section_count - 1), 0, keepdims=False
        )[0]
        step = jnp.clip(tick - section_pos, 0, TICKS - 1)
        from_fresh = fresh_docs[step, plan[step, replica_pos]]
        return jnp.where(section_pos > tick, from_arrivals, from_fresh)[None, :]

    own_kv = [key_weight[0], value_weight[0]]
    pair_kv = own_kv
    for bit in range(bit_count):
        low_side = tensor_pos >> bit & 1 == 0
        partners = [exchange(block, "tensor", 1 << bit) for block in pair_kv]
        pair_kv = [
            jnp.where(
                low_side,
                jnp.concatenate([block, partner], -1),
                jnp.concatenate([partner, block], -1),
            )
            for block, partner in zip(pair_kv, partners)
        ]
    head_cols = pair_kv[0].shape[1]
    kv_heads = head_cols // HEAD_SIZE
    own_weight = jnp.concatenate([query_weight[0], *pair_kv], 1)
    out_x, weight_x = [exchange(weight, "dp", 2) for weight in (w_out[0], own_weight)]
    out_sibling, weight_sibling = [exchange(weight, "dp", 1) for weight in (w_out[0], own_weight)]
    grad_in = jnp.where(
        section_pos == section_count - 1,
        loss_grad[0, 0],
        shifted(returning[0, 0], "section", -1),
    )
    new_docs = [forward_documents(tick) for tick in range(TICKS)]
    old_docs = [stash_docs[tick, 0, 0][None, :] for tick in range(TICKS)]
    balanced = balance(fresh[:, 0], own_weight, grad_in, *new_docs, *old_docs)
    out_x = tie(out_x, balanced)
    out_parts = [w_out[0], out_sibling, out_x, exchange(out_x, "dp", 1)]

    first_in = balanced[0]
    if section_count > TICKS:
        first_in = jnp.where(section_pos == 0, first_in, shifted(arrivals[0, 0], "section", 1))
    gain_rows = jnp.stack(split_float(gain[0]) + [jnp.zeros((width,), BF16)] * 13)
    early = jnp.concatenate([stash[0, 0, 0], stash[1, 0, 0], gain_rows], 0)
    early = lax.all_gather(early, "tensor")

    def early_block(index):
        group = tensor_count // replicas
        block = lax.dynamic_slice_in_dim(early, index * group, group, 0)
        return block.transpose(1, 0, 2).reshape(early.shape[1], block_rows)

    def gain_of(block):
        return sum(block[-16 + i : -15 + i].astype(F32) for i in range(3))

    narrow = [shape(length, block_rows, BF16)] * replicas
    if paired:
        sent = call(
            [
                Work(spread_two_body, [(balanced, (0,)), (balanced, (1,))]),
                Work(
                    turned_two_body, [(loss_grad, (0, 0)), (loss_grad, (1, 0))], [out_parts], picks
                ),
            ],
            narrow * 2,
            (),
            last,
        )
        firsts = swap(sent[:replicas])
        seconds = swap(sent[replicas:])
        sent = call(
            [Work(functools.partial(turned_body, 1), [grad_in], [out_parts], picks), None],
            narrow,
            firsts[1:3],
            last,
        )
        heads = swap(sent, every[:1])
    else:
        firsts = gather(first_in)
        heads, _ = whole_scatter([grad_in], [out_parts])
    mine = jnp.stack(firsts)

    saved = TICKS * length
    squares = jnp.sum(jnp.square(early[:, :saved].astype(F32)), (0, 2))
    blocks = [early_block(replica_pos ^ mask) for mask in range(replicas)]
    turns = [gain_of(block) for block in blocks]
    rows = [
        (block[:saved].astype(F32) * gain_block).astype(BF16)
        for block, gain_block in zip(blocks, turns)
    ]
    squares = jnp.concatenate([squares, jnp.sum(jnp.square(mine.astype(F32)), (0, 2))])[:, None]
    for mask in range(replicas):
        block = lax.dynamic_index_in_dim(mine, which[mask], 0, keepdims=False).astype(F32)
        rows[mask] = jnp.concatenate([rows[mask], (block * turns[mask]).astype(BF16)], 0)
    gains = [gain_of(early_block(mask ^ shift)) for mask in range(replicas)]
    (total,) = call(
        Work(
            functools.partial(sum_body, 2), rows[:2], [[own_weight, weight_sibling]], fixed(0, 1)
        ),
        [shape(saved + length, own_weight.shape[1])],
        seconds[1:] if paired else (),
    )
    weight_x = tie(weight_x, total, rows[2], rows[3], squares, *heads[1:])
    parts = [own_weight, weight_sibling, weight_x, exchange(weight_x, "dp", 1)]
    states = call(
        Work(last_sum_body, [rows[2], rows[3], total, squares], [parts[2:]], fixed(0, 1)),
        [shape(length, own_weight.shape[1], BF16)] * 3,
    )
    old_squares = [squares[tick * length : (tick + 1) * length] for tick in range(TICKS)]
    wide = [shape(length, block_rows + HEAD_SIZE, BF16)] * replicas
    sent_type = [shape(length, width, BF16), shape(1, width)]

    def mix_work(state, documents):
        return Work(functools.partial(mix_body, kv_heads), [state, documents])

    def project_mix_work(blocks):
        return Work(
            functools.partial(project_mix_body, kv_heads),
            [*blocks, *gains, new_docs[1]],
            [parts],
            picks,
        )

    def back_work(state, documents, terms, *shares):
        return Work(
            functools.partial(back_body, kv_heads, len(terms)),
            [state, documents, *terms, *shares],
            [parts],
            picks,
        )

    def out_work(hidden, blocks):
        return Work(out_body, [hidden, *blocks], [out_parts], picks)

    def result_work(tick, grad, terms, sides=()):
        return Work(
            functools.partial(result_body, len(terms)),
            [(stash, (tick, 0, 0)), grad, gain, old_squares[tick], *terms, *sides],
        )

    if paired:
        swapped = swap(
            call(
                [mix_work(states[2], new_docs[0]), back_work(states[0], old_docs[0], firsts)],
                wide,
                (),
                last,
            )
        )
        apart_sent = call(
            [project_mix_work(seconds), back_work(states[1], old_docs[1], seconds)],
            wide,
            swapped[1:2],
            last,
        )
        apart = swap(apart_sent)
        sent, gain_0 = call(
            [out_work(firsts[0], swapped), result_work(0, (loss_grad, (0, 0)), swapped)],
            sent_type,
            apart_sent[:1],
            last,
        )
        arrived = exchange(sent, "section", 1)
        swapped = swap(
            call(
                [
                    Work(functools.partial(turned_body, 1), [arrived], [out_parts], picks),
                    Work(spread_body, [arrived]),
                ],
                narrow,
                apart[1:],
                last,
            )
        )
        saved_blocks = jnp.stack([early_block(tensor_pos ^ mask)[:length] for mask in range(replicas)])
        (shares,) = call(
            [
                Work(
                    functools.partial(gain_body, kv_heads, replicas),
                    [states[0], old_docs[0], old_squares[0], saved_blocks, *heads],
                    [parts],
                    picks,
                ),
                Work(lambda ref: spread(jnp.zeros_like(ref), [ref]), []),
            ],
            [shape(replicas, block_rows)],
            swapped[1:2],
            last,
        )
        swapped = swap(
            call(
                [back_work(states[1], old_docs[1], swapped, shares), project_mix_work(swapped)],
                [shape(length + 16, block_rows + HEAD_SIZE, BF16)] * replicas,
                (),
                last,
            )
        )
        early_out, gain_1 = call(
            [out_work(seconds[0], apart), result_work(1, (loss_grad, (1, 0)), apart)],
            sent_type,
            swapped[1:2],
            last,
        )
        late_out, gain_3 = call(
            [result_work(1, arrived, swapped), out_work(arrived, swapped)],
            sent_type,
            [early_out],
            last,
        )
        outgoing = jnp.where(last == 1, late_out, early_out)
        going_back = jnp.where(last == 1, early_out, late_out)
        gain_total = gain_0 + gain_1 + gain_3
    else:
        grad_groups = [parts]
        if bit_count:
            grad_groups = [gather_dp(query_weight[0]), gather_dp(jnp.concatenate(own_kv, 1))]
        gain_total = jnp.zeros((1, width), F32)
        hidden = first_in
        for tick in range(TICKS):
            if tick:
                hidden = jnp.where(first == 1, balanced[1], shifted(outgoing, "section", 1))
                grad_in = jnp.where(
                    last == 1, loss_grad[1, 0], shifted(going_back, "section", -1)
                )
                mixed_work = project_mix_work(gather(hidden))
                heads, _ = whole_scatter([grad_in], [out_parts])
            else:
                mixed_work = mix_work(states[2], new_docs[0])
            (mixed,) = call(mixed_work, [shape(length, query_cols, BF16)])
            (outgoing,) = call(out_work(hidden, gather(mixed)), sent_type[:1])
            query_grad, kv_grad, aside = call(
                Work(
                    functools.partial(heads_body, kv_heads, len(heads)),
                    [states[tick], old_docs[tick], *heads],
                ),
                [
                    shape(length, query_cols, BF16),
                    shape(length, 2 * head_cols, F32 if bit_count else BF16),
                    shape(length, HEAD_SIZE, BF16),
                ],
            )
            grads = [jnp.concatenate([query_grad, kv_grad.astype(BF16)], 1)]
            if bit_count:
                kv_grad = jnp.stack([kv_grad[:, :head_cols], kv_grad[:, head_cols:]])
                for bit in reversed(range(bit_count)):
                    half = kv_grad.shape[-1] // 2
                    low_side = tensor_pos >> bit & 1 == 0
                    keep = jnp.where(low_side, kv_grad[..., :half], kv_grad[..., half:])
                    outward = jnp.where(low_side, kv_grad[..., half:], kv_grad[..., :half])
                    kv_grad = keep + exchange(outward.astype(BF16), "tensor", 1 << bit).astype(F32)
                grads = [query_grad, jnp.concatenate([kv_grad[0], kv_grad[1]], 1).astype(BF16)]
            terms, sides = whole_scatter(grads, grad_groups, aside)
            going_back, gain_term = call(result_work(tick, grad_in, terms, sides), sent_type)
            gain_total = gain_total + gain_term
    gain_total = gain_total + exchange(gain_total, "dp", 1)
    gain_total = gain_total + exchange(gain_total, "dp", 2)
    gain_grad = gain_total / math.sqrt(TICKS * replicas * length)
    return (outgoing[None, None], going_back[None, None], gain_grad)


def solution(mesh):
    return jax.shard_map(
        local,
        mesh=mesh,
        in_specs=(
            P("section", "dp", None, "tensor"),
            P(None, "dp", None, "tensor"),
            P(None, "section", "dp", None, "tensor"),
            P("section", "dp", None, "tensor"),
            P(None, "dp", None, "tensor"),
            P("section", "tensor"),
            P("section", "dp", "tensor"),
            P("section", "dp", "tensor"),
            P("section", "dp", "tensor"),
            P("section", "dp", "tensor"),
            P(),
            P(),
            P(None, "dp", None),
            P(None, "section", "dp", None),
        ),
        out_specs=(
            P("section", "dp", None, "tensor"),
            P("section", "dp", None, "tensor"),
            P("section", "tensor"),
        ),
        check_vma=False,
    )
```

```python
import functools
import math

import jax
import jax.numpy as jnp
from jax import lax
from jax.experimental import pallas as pl
from jax.experimental.pallas import tpu as pltpu
from jax.sharding import PartitionSpec as P

MODEL_WIDTH = 4096
QUERY_HEADS = 32
KEY_VALUE_HEADS = 8
HEAD_SIZE = 128
TICKS = 2
NORM_EPS = 1e-05
F32 = jnp.float32
BF16 = jnp.bfloat16


NEAR = (((1,), (1,)), ((), ()))
FIRST = (((0,), (0,)), ((), ()))
CHUNKS = 2
VMEM = 22 * 2**20
SMEM_SPEC = pl.BlockSpec(memory_space=pltpu.SMEM)
ANY_SPEC = pl.BlockSpec(memory_space=pl.ANY)
VMEM_SPEC = pl.BlockSpec(memory_space=pltpu.VMEM)


def exchange(block, axis, mask):
    count = lax.axis_size(axis)
    return lax.ppermute(block, axis, [(i, i ^ mask) for i in range(count)])


def exchange_tensor(block, mask, sections):
    count = lax.axis_size("tensor")
    return lax.ppermute(
        block,
        ("section", "tensor"),
        [(s * count + i, s * count + (i ^ mask)) for s in sections for i in range(count)],
    )


def shifted(value, axis, steps):
    count = lax.axis_size(axis)
    leading, last = (max(0, -steps), min(count, count - steps))
    return lax.ppermute(value, axis, [(source, source + steps) for source in range(leading, last)])


def dot(left, right, contract=(((1,), (0,)), ((), ()))):
    return lax.dot_general(left, right, contract, preferred_element_type=F32)


def shape(rows, cols, dtype=F32):
    return jax.ShapeDtypeStruct((rows, cols), dtype)


class Work:
    def __init__(self, body, args, groups=(), which=None):
        self.body, self.groups = body, groups
        self.count = 0 if which is None else which.shape[0]
        pairs = [arg if isinstance(arg, tuple) else (arg, ()) for arg in args]
        self.index = [index for _, index in pairs]
        self.plain = len(args)
        self.args = [array for array, _ in pairs] + [part for parts in groups for part in parts]
        self.specs = [ANY_SPEC] * len(self.args)
        dims = [
            tuple(i.stop - i.start for i in index if isinstance(i, slice))
            + array.shape[len(index) :]
            for array, index in pairs
        ]
        self.scratch = [
            pltpu.VMEM(size, array.dtype) for size, (array, _) in zip(dims, pairs)
        ] + [pltpu.SemaphoreType.DMA((max(1, len(args)),))]
        if groups:
            self.args.append(which)
            self.specs.append(SMEM_SPEC)
        self.loading = [pltpu.VMEM((self.count,) + parts[0].shape, BF16) for parts in groups]
        if groups:
            self.loading.append(pltpu.SemaphoreType.DMA((len(groups), self.count, CHUNKS)))

    def run(self, args, outs, scratch):
        plain, rest = args[: self.plain], list(args[self.plain :])
        held, sems, loading = scratch[: self.plain], scratch[self.plain], scratch[self.plain + 1 :]
        copies = [
            pltpu.make_async_copy(ref.at[index] if index else ref, copy, sems.at[i])
            for i, (ref, index, copy) in enumerate(zip(plain, self.index, held))
        ]
        for copy in copies:
            copy.start()
        loader = []
        if self.groups:
            groups = [[rest.pop(0) for _ in parts] for parts in self.groups]
            loader = [Loader(rest[0], groups, loading[:-1], loading[-1], self.count)]
        for copy in copies:
            copy.wait()
        return self.body(*loader, *held, *outs)


class Loader:
    def __init__(self, which_ref, groups, buffers, sems, count):
        self.groups, self.buffers, self.sems, self.count = groups, buffers, sems, count
        for i in range(count):
            for chunk in range(CHUNKS):
                for group, parts in enumerate(groups):
                    for k, part in enumerate(parts):
                        pl.when(which_ref[i] == k)(self.copy(part, group, i, chunk).start)

    def copy(self, part, group, i, chunk):
        rows = part.shape[0] // CHUNKS
        at = pl.ds(chunk * rows, rows)
        return pltpu.make_async_copy(
            part.at[at], self.buffers[group].at[i, at], self.sems.at[group, i, chunk]
        )

    def rows(self, group, i, chunk):
        part = self.groups[group][0]
        self.copy(part, group, i, chunk).wait()
        count = part.shape[0] // CHUNKS
        at = slice(chunk * count, (chunk + 1) * count)
        return at, self.buffers[group][i, at]


def call(works, outs, after=(), flag=None):
    works = works if isinstance(works, list) else [works]
    flags = [] if flag is None else [flag.reshape(1)]
    sizes = [len(work.args) if work else 0 for work in works]
    loads = [work.loading for work in works if work and work.loading]
    scratch = [item for work in works if work for item in work.scratch] + (loads or [[]])[0]
    extra = len(after) + len(flags)

    def body(*refs):
        refs = list(refs)
        take = lambda n: [refs.pop(0) for _ in range(n)]
        flag_ref = take(len(flags))
        operands = [take(size) for size in sizes]
        take(len(after))
        results = take(len(outs))
        for number, work in enumerate(works):
            if work:
                held = take(len(work.scratch))
                loading = refs[len(refs) - len(work.loading) :]
                run = functools.partial(work.run, operands[number], results, held + loading)
                if flag_ref:
                    pl.when(flag_ref[0][0] == number)(run)
                else:
                    run()

    return pl.pallas_call(
        body,
        in_specs=[SMEM_SPEC] * len(flags)
        + [spec for work in works if work for spec in work.specs]
        + [ANY_SPEC] * len(after),
        out_specs=[VMEM_SPEC] * len(outs),
        out_shape=list(outs),
        scratch_shapes=scratch,
        compiler_params=pltpu.CompilerParams(vmem_limit_bytes=VMEM),
        cost_estimate=pl.CostEstimate(flops=1024, bytes_accessed=1024, transcendentals=0),
    )(*flags, *[arg for work in works if work for arg in work.args], *after)


def tie(value, *after):
    def body(*refs):
        pass

    return pl.pallas_call(
        body,
        in_specs=[ANY_SPEC] * (1 + len(after)),
        out_specs=ANY_SPEC,
        out_shape=jax.ShapeDtypeStruct(value.shape, value.dtype),
        input_output_aliases={0: 0},
        cost_estimate=pl.CostEstimate(flops=0, bytes_accessed=0, transcendentals=0),
    )(value, *after)


def summed(loader, blocks, start=None):
    totals = []
    for group in range(len(loader.groups)):
        total = start
        for i, block in enumerate(blocks):
            for chunk in range(CHUNKS):
                at, rows = loader.rows(group, i, chunk)
                term = dot(block[:, at], rows)
                total = term if total is None else total + term
        totals.append(total)
    return totals[0] if len(totals) == 1 else jnp.concatenate(totals, 1)


def inverse_of(squares):
    return lax.rsqrt(squares / MODEL_WIDTH + NORM_EPS)


def sum_body(count, loader, *refs):
    blocks = [ref[...] for ref in refs[:count]]
    refs[-1][...] = summed(loader, blocks, refs[count][...] if len(refs) > count + 1 else None)


def last_sum_body(loader, first_ref, second_ref, before_ref, squares_ref, *outs):
    total = summed(loader, [first_ref[...], second_ref[...]], before_ref[...])
    rows = (total * inverse_of(squares_ref[...])).astype(BF16)
    length = outs[0].shape[0]
    for i, out in enumerate(outs):
        out[...] = rows[i * length : (i + 1) * length]


def stacked(value, first, per_key):
    return jnp.concatenate(
        [value[:, (first + a) * HEAD_SIZE : (first + a + 1) * HEAD_SIZE] for a in range(per_key)], 0
    )


def allowed_pairs(docs_ref, per_key):
    length = docs_ref.shape[1]
    docs = jnp.broadcast_to(docs_ref[...].astype(F32), (length, length))
    down = lax.broadcasted_iota(jnp.int32, (length, length), 0)
    across = lax.broadcasted_iota(jnp.int32, (length, length), 1)
    allowed = jnp.where(jnp.logical_and(docs.T == docs, down >= across), 1.0, 0.0)
    return jnp.concatenate([allowed] * per_key, 0) > 0.5


def masked_probs(rows, keys, allowed):
    scores = dot(rows, keys, NEAR) * HEAD_SIZE ** (-0.5)
    raised = jnp.where(allowed, jnp.exp(scores), 0.0)
    return raised / jnp.sum(raised, axis=-1, keepdims=True)


def mix(kv_heads, rows, docs_ref):
    length = rows.shape[0]
    query_cols = rows.shape[1] - 2 * kv_heads * HEAD_SIZE
    per_key = query_cols // (kv_heads * HEAD_SIZE)
    allowed = allowed_pairs(docs_ref, per_key)
    out = []
    for head in range(kv_heads):
        key_at = query_cols + head * HEAD_SIZE
        value_at = key_at + kv_heads * HEAD_SIZE
        query = stacked(rows, head * per_key, per_key)
        probs = masked_probs(query, rows[:, key_at : key_at + HEAD_SIZE], allowed)
        mixed = dot(probs.astype(BF16), rows[:, value_at : value_at + HEAD_SIZE]).astype(BF16)
        out += [mixed[a * length : (a + 1) * length] for a in range(per_key)]
    return jnp.concatenate(out, 1)


def two_lanes(value):
    high = value.astype(BF16).astype(F32)
    lane = lax.broadcasted_iota(jnp.int32, (value.shape[0], HEAD_SIZE), 1)
    return jnp.where(lane == 0, high, jnp.where(lane == 1, value - high, 0.0)).astype(BF16)


def head_grads(kv_heads, rows, docs_ref, terms):
    length = rows.shape[0]
    query_cols = rows.shape[1] - 2 * kv_heads * HEAD_SIZE
    per_key = query_cols // (kv_heads * HEAD_SIZE)
    allowed = allowed_pairs(docs_ref, per_key)
    total = terms[0][...].astype(F32)
    for term in terms[1:]:
        total = total + term[...].astype(F32)
    grads = total.astype(BF16)
    row_dot = jnp.zeros((length, 1), F32)
    query_grads, key_grads, value_grads = [], [], []
    for head in range(kv_heads):
        key_at = query_cols + head * HEAD_SIZE
        value_at = key_at + kv_heads * HEAD_SIZE
        query = stacked(rows, head * per_key, per_key)
        keys = rows[:, key_at : key_at + HEAD_SIZE]
        values = rows[:, value_at : value_at + HEAD_SIZE]
        probs = masked_probs(query, keys, allowed)
        grad = stacked(grads, head * per_key, per_key)
        prob_grad = dot(grad, values, NEAR)
        inner = jnp.sum(probs * prob_grad, axis=-1, keepdims=True)
        score_grad = (probs * (prob_grad - inner) * HEAD_SIZE ** (-0.5)).astype(BF16)
        query_grad = dot(score_grad, keys)
        key_grad = dot(score_grad, query, FIRST)
        value_grad = dot(probs.astype(BF16), grad, FIRST)
        products = jnp.sum(query_grad * query.astype(F32), axis=-1, keepdims=True)
        for a in range(per_key):
            at = slice(a * length, (a + 1) * length)
            query_grads.append(query_grad[at].astype(BF16))
            row_dot = row_dot + products[at]
        row_dot = row_dot + jnp.sum(key_grad * keys.astype(F32), axis=-1, keepdims=True)
        row_dot = row_dot + jnp.sum(value_grad * values.astype(F32), axis=-1, keepdims=True)
        key_grads.append(key_grad)
        value_grads.append(value_grad)
    return query_grads, key_grads + value_grads, two_lanes(row_dot)


def turned(loader, lefts, outs):
    for i, out in enumerate(outs):
        for chunk in range(CHUNKS):
            total = 0.0
            for group, left in enumerate(lefts):
                at, rows = loader.rows(group, i, chunk)
                total = total + dot(left, rows, NEAR)
            out[: total.shape[0], at] = total.astype(BF16)


def spread(block, outs):
    for out in outs:
        out[: block.shape[0], : block.shape[1]] = block


def spread_body(block_ref, *outs):
    spread(block_ref[...], outs)


def spread_two_body(first_ref, second_ref, *outs):
    spread(first_ref[...], outs[: len(outs) // 2])
    spread(second_ref[...], outs[len(outs) // 2 :])


def turned_two_body(loader, first_ref, second_ref, *outs):
    length = first_ref.shape[0]
    left = jnp.concatenate([first_ref[...], second_ref[...]], 0)
    for i in range(loader.count):
        for chunk in range(CHUNKS):
            at, rows = loader.rows(0, i, chunk)
            total = dot(left, rows, NEAR).astype(BF16)
            outs[i][:, at] = total[:length]
            outs[loader.count + i][:, at] = total[length:]


def turned_body(count, loader, *refs):
    turned(loader, [ref[...] for ref in refs[:count]], refs[count:])


def mix_body(kv_heads, rows_ref, docs_ref, *outs):
    spread(mix(kv_heads, rows_ref[...], docs_ref), outs)


def project_mix_body(kv_heads, loader, *refs):
    count = loader.count
    blocks, gains = refs[:count], refs[count : 2 * count]
    docs_ref, outs = refs[2 * count], refs[2 * count + 1 :]
    width = gains[0].shape[1]
    squares, scaled = 0.0, []
    for block, gain in zip(blocks, gains):
        block = block[:, :width].astype(F32)
        squares = squares + jnp.sum(block * block, axis=-1, keepdims=True)
        scaled.append((block * gain[...]).astype(BF16))
    rows = (summed(loader, scaled) * inverse_of(squares)).astype(BF16)
    spread(mix(kv_heads, rows, docs_ref), outs)


def back_body(kv_heads, count, loader, rows_ref, docs_ref, *refs):
    length = rows_ref.shape[0]
    terms, outs = refs[:count], refs[-loader.count :]
    query_grads, kv_grads, lanes = head_grads(kv_heads, rows_ref[...], docs_ref, terms)
    left = jnp.concatenate(query_grads + [grad.astype(BF16) for grad in kv_grads], 1)
    turned(loader, [left], outs)
    for i, out in enumerate(outs):
        out[:length, -HEAD_SIZE:] = lanes
        if out.shape[0] > length:
            share = refs[count][i : i + 1]
            high = share.astype(BF16).astype(F32)
            middle = (share - high).astype(BF16).astype(F32)
            row = lax.broadcasted_iota(jnp.int32, (out.shape[0] - length, share.shape[1]), 0)
            low = jnp.where(row == 2, share - high - middle, 0.0)
            out[length:, : share.shape[1]] = jnp.where(
                row == 0, high, jnp.where(row == 1, middle, low)
            ).astype(BF16)


def gain_body(kv_heads, count, loader, rows_ref, docs_ref, squares_ref, hidden_ref, *refs):
    terms, out = refs[:count], refs[count]
    query_grads, kv_grads, _ = head_grads(kv_heads, rows_ref[...], docs_ref, terms)
    left = jnp.concatenate(query_grads + [grad.astype(BF16) for grad in kv_grads], 1)
    inverse = inverse_of(squares_ref[...])
    for i in range(loader.count):
        for chunk in range(CHUNKS):
            at, rows = loader.rows(0, i, chunk)
            term = dot(left, rows, NEAR) * (hidden_ref[i, :, at].astype(F32) * inverse)
            out[i : i + 1, at] = jnp.sum(term, axis=0, keepdims=True)


def heads_body(kv_heads, count, rows_ref, docs_ref, *refs):
    terms, (query_ref, kv_ref, lanes_ref) = refs[:count], refs[count:]
    query_grads, kv_grads, lanes = head_grads(kv_heads, rows_ref[...], docs_ref, terms)
    query_ref[...] = jnp.concatenate(query_grads, 1)
    kv_ref[...] = jnp.concatenate(kv_grads, 1).astype(kv_ref.dtype)
    lanes_ref[...] = lanes


def out_body(loader, hidden_ref, *refs):
    blocks, outs = refs[: loader.count], refs[loader.count :]
    length, width = hidden_ref.shape[0], loader.groups[0][0].shape[0]
    total = summed(loader, [block[:length, :width] for block in blocks])
    outs[0][...] = (hidden_ref[...].astype(F32) + total).astype(BF16)
    for out in outs[1:]:
        out[...] = jnp.zeros_like(out)


def result_body(count, hidden_ref, grad_ref, gain_ref, squares_ref, *refs):
    terms, sides, (result_ref, term_ref) = refs[:count], refs[count:-2], refs[-2:]
    length, width = hidden_ref.shape
    normed_grad = sum(term[:length, :width].astype(F32) for term in terms)
    lanes = sum(side[:length, -HEAD_SIZE:].astype(F32) for side in sides or terms)
    inverse = inverse_of(squares_ref[...])
    row_dot = (lanes[:, :1] + lanes[:, 1:2]) / inverse
    hidden = hidden_ref[...].astype(F32)
    result_ref[...] = (
        grad_ref[...].astype(F32)
        + inverse * (normed_grad * gain_ref[...])
        - hidden * (inverse * inverse * inverse * row_dot / MODEL_WIDTH)
    ).astype(BF16)
    total = jnp.sum(normed_grad * hidden * inverse, axis=0, keepdims=True)
    if terms[0].shape[0] > length:
        total = total + sum(
            jnp.sum(term[length:, :width].astype(F32), axis=0, keepdims=True) for term in terms
        )
    term_ref[...] = total


def split_float(value):
    high = lax.reduce_precision(value, 8, 7)
    middle = lax.reduce_precision(value - high, 8, 7)
    return [high.astype(BF16), middle.astype(BF16), (value - high - middle).astype(BF16)]


def local(
    arrivals,
    fresh,
    stash,
    returning,
    loss_grad,
    gain,
    query_weight,
    key_weight,
    value_weight,
    w_out,
    plan,
    fresh_docs,
    arrival_docs,
    stash_docs,
):
    tensor_count = lax.axis_size("tensor")
    section_count = lax.axis_size("section")
    replicas = lax.axis_size("dp")
    tensor_pos = lax.axis_index("tensor")
    section_pos = lax.axis_index("section")
    replica_pos = lax.axis_index("dp")
    length, width = arrivals.shape[2:]
    heads_here = QUERY_HEADS // tensor_count
    group_width = QUERY_HEADS // KEY_VALUE_HEADS
    share_count = max(1, group_width // heads_here)
    bit_count = share_count.bit_length() - 1
    query_cols = heads_here * HEAD_SIZE
    block_rows = query_weight.shape[1]
    every = range(section_count)
    paired = tensor_count == replicas and section_count == 2
    shift = tensor_pos if paired else 0
    first = (section_pos == 0).astype(jnp.int32)
    last = (section_pos == section_count - 1).astype(jnp.int32)
    which = [(replica_pos ^ mask ^ shift).astype(jnp.int32) for mask in range(replicas)]
    picks = jnp.stack(which)

    def fixed(*masks):
        return jnp.array(masks, jnp.int32)

    def gather_dp(weight):
        other = exchange(weight, "dp", 2)
        return [weight, exchange(weight, "dp", 1), other, exchange(other, "dp", 1)]

    def gather(block):
        whole = lax.all_gather(block, "tensor", axis=1, tiled=True)
        return jnp.split(whole, replicas, 1)

    def swap(blocks, sections=every):
        far, middle, near = [exchange_tensor(blocks[mask], mask, sections) for mask in (3, 2, 1)]
        return [blocks[0], near, middle, far]

    def whole_scatter(lefts, groups, aside=None):
        part = call(
            Work(functools.partial(turned_body, len(lefts)), lefts, groups, picks),
            [shape(length, block_rows, BF16)] * replicas,
        )
        part = jnp.concatenate(part, 1)
        terms = [lax.psum_scatter(part, "tensor", scatter_dimension=1, tiled=True)]
        if aside is None:
            return terms, []
        total = lax.psum(aside[:, :2].astype(F32), "tensor")
        rest = jnp.zeros((length, HEAD_SIZE - 2), F32)
        return terms, [jnp.concatenate([total, rest], 1)]

    def balance(rows, *after):
        sibling = exchange(rows, "dp", 1)
        asked = plan[:, replica_pos ^ 2][:, None, None]
        source = plan[:, replica_pos][:, None, None]
        far = exchange(tie(jnp.where(asked == replica_pos, rows, sibling), *after), "dp", 2)
        return jnp.where(
            source == replica_pos, rows, jnp.where(source == replica_pos ^ 1, sibling, far)
        )

    def forward_documents(tick):
        from_arrivals = lax.dynamic_index_in_dim(
            arrival_docs, jnp.clip(section_pos - tick - 1, 0, section_count - 1), 0, keepdims=False
        )[0]
        step = jnp.clip(tick - section_pos, 0, TICKS - 1)
        from_fresh = fresh_docs[step, plan[step, replica_pos]]
        return jnp.where(section_pos > tick, from_arrivals, from_fresh)[None, :]

    own_kv = [key_weight[0], value_weight[0]]
    pair_kv = own_kv
    for bit in range(bit_count):
        low_side = tensor_pos >> bit & 1 == 0
        partners = [exchange(block, "tensor", 1 << bit) for block in pair_kv]
        pair_kv = [
            jnp.where(
                low_side,
                jnp.concatenate([block, partner], -1),
                jnp.concatenate([partner, block], -1),
            )
            for block, partner in zip(pair_kv, partners)
        ]
    head_cols = pair_kv[0].shape[1]
    kv_heads = head_cols // HEAD_SIZE
    own_weight = jnp.concatenate([query_weight[0], *pair_kv], 1)
    out_x, weight_x = [exchange(weight, "dp", 2) for weight in (w_out[0], own_weight)]
    out_sibling, weight_sibling = [exchange(weight, "dp", 1) for weight in (w_out[0], own_weight)]
    grad_in = jnp.where(
        section_pos == section_count - 1,
        loss_grad[0, 0],
        shifted(returning[0, 0], "section", -1),
    )
    new_docs = [forward_documents(tick) for tick in range(TICKS)]
    old_docs = [stash_docs[tick, 0, 0][None, :] for tick in range(TICKS)]
    balanced = balance(fresh[:, 0], own_weight, grad_in, *new_docs, *old_docs)
    out_x = tie(out_x, balanced)
    out_parts = [w_out[0], out_sibling, out_x, exchange(out_x, "dp", 1)]

    first_in = balanced[0]
    if section_count > TICKS:
        first_in = jnp.where(section_pos == 0, first_in, shifted(arrivals[0, 0], "section", 1))
    gain_rows = jnp.stack(split_float(gain[0]) + [jnp.zeros((width,), BF16)] * 13)
    early = jnp.concatenate([stash[0, 0, 0], stash[1, 0, 0], gain_rows], 0)
    early = lax.all_gather(early, "tensor")

    def early_block(index):
        group = tensor_count // replicas
        block = lax.dynamic_slice_in_dim(early, index * group, group, 0)
        return block.transpose(1, 0, 2).reshape(early.shape[1], block_rows)

    def gain_of(block):
        return sum(block[-16 + i : -15 + i].astype(F32) for i in range(3))

    narrow = [shape(length, block_rows, BF16)] * replicas
    if paired:
        sent = call(
            [
                Work(spread_two_body, [(balanced, (0,)), (balanced, (1,))]),
                Work(
                    turned_two_body, [(loss_grad, (0, 0)), (loss_grad, (1, 0))], [out_parts], picks
                ),
            ],
            narrow * 2,
            (),
            last,
        )
        firsts = swap(sent[:replicas])
        seconds = swap(sent[replicas:])
        sent = call(
            [Work(functools.partial(turned_body, 1), [grad_in], [out_parts], picks), None],
            narrow,
            firsts[1:3],
            last,
        )
        heads = swap(sent, every[:1])
    else:
        firsts = gather(first_in)
        heads, _ = whole_scatter([grad_in], [out_parts])
    mine = jnp.stack(firsts)

    saved = TICKS * length
    squares = jnp.sum(jnp.square(early[:, :saved].astype(F32)), (0, 2))
    blocks = [early_block(replica_pos ^ mask) for mask in range(replicas)]
    turns = [gain_of(block) for block in blocks]
    rows = [
        (block[:saved].astype(F32) * gain_block).astype(BF16)
        for block, gain_block in zip(blocks, turns)
    ]
    squares = jnp.concatenate([squares, jnp.sum(jnp.square(mine.astype(F32)), (0, 2))])[:, None]
    for mask in range(replicas):
        block = lax.dynamic_index_in_dim(mine, which[mask], 0, keepdims=False).astype(F32)
        rows[mask] = jnp.concatenate([rows[mask], (block * turns[mask]).astype(BF16)], 0)
    gains = [gain_of(early_block(mask ^ shift)) for mask in range(replicas)]
    (total,) = call(
        Work(
            functools.partial(sum_body, 2), rows[:2], [[own_weight, weight_sibling]], fixed(0, 1)
        ),
        [shape(saved + length, own_weight.shape[1])],
        seconds[1:] if paired else (),
    )
    weight_x = tie(weight_x, total, rows[2], rows[3], squares, *heads[1:])
    parts = [own_weight, weight_sibling, weight_x, exchange(weight_x, "dp", 1)]
    states = call(
        Work(last_sum_body, [rows[2], rows[3], total, squares], [parts[2:]], fixed(0, 1)),
        [shape(length, own_weight.shape[1], BF16)] * 3,
    )
    old_squares = [squares[tick * length : (tick + 1) * length] for tick in range(TICKS)]
    wide = [shape(length, block_rows + HEAD_SIZE, BF16)] * replicas
    sent_type = [shape(length, width, BF16), shape(1, width)]

    def mix_work(state, documents):
        return Work(functools.partial(mix_body, kv_heads), [state, documents])

    def project_mix_work(blocks):
        return Work(
            functools.partial(project_mix_body, kv_heads),
            [*blocks, *gains, new_docs[1]],
            [parts],
            picks,
        )

    def back_work(state, documents, terms, *shares):
        return Work(
            functools.partial(back_body, kv_heads, len(terms)),
            [state, documents, *terms, *shares],
            [parts],
            picks,
        )

    def out_work(hidden, blocks):
        return Work(out_body, [hidden, *blocks], [out_parts], picks)

    def result_work(tick, grad, terms, sides=()):
        return Work(
            functools.partial(result_body, len(terms)),
            [(stash, (tick, 0, 0)), grad, gain, old_squares[tick], *terms, *sides],
        )

    if paired:
        swapped = swap(
            call(
                [mix_work(states[2], new_docs[0]), back_work(states[0], old_docs[0], firsts)],
                wide,
                (),
                last,
            )
        )
        apart_sent = call(
            [project_mix_work(seconds), back_work(states[1], old_docs[1], seconds)],
            wide,
            swapped[1:2],
            last,
        )
        apart = swap(apart_sent)
        sent, gain_0 = call(
            [out_work(firsts[0], swapped), result_work(0, (loss_grad, (0, 0)), swapped)],
            sent_type,
            apart_sent[:1],
            last,
        )
        arrived = exchange(sent, "section", 1)
        swapped = swap(
            call(
                [
                    Work(functools.partial(turned_body, 1), [arrived], [out_parts], picks),
                    Work(spread_body, [arrived]),
                ],
                narrow,
                apart[1:],
                last,
            )
        )
        saved_blocks = jnp.stack([early_block(tensor_pos ^ mask)[:length] for mask in range(replicas)])
        (shares,) = call(
            [
                Work(
                    functools.partial(gain_body, kv_heads, replicas),
                    [states[0], old_docs[0], old_squares[0], saved_blocks, *heads],
                    [parts],
                    picks,
                ),
                Work(lambda ref: spread(jnp.zeros_like(ref), [ref]), []),
            ],
            [shape(replicas, block_rows)],
            swapped[1:2],
            last,
        )
        swapped = swap(
            call(
                [back_work(states[1], old_docs[1], swapped, shares), project_mix_work(swapped)],
                [shape(length + 16, block_rows + HEAD_SIZE, BF16)] * replicas,
                (),
                last,
            )
        )
        early_out, gain_1 = call(
            [out_work(seconds[0], apart), result_work(1, (loss_grad, (1, 0)), apart)],
            sent_type,
            swapped[1:2],
            last,
        )
        late_out, gain_3 = call(
            [result_work(1, arrived, swapped), out_work(arrived, swapped)],
            sent_type,
            [early_out],
            last,
        )
        outgoing = jnp.where(last == 1, late_out, early_out)
        going_back = jnp.where(last == 1, early_out, late_out)
        gain_total = gain_0 + gain_1 + gain_3
    else:
        grad_groups = [parts]
        if bit_count:
            grad_groups = [gather_dp(query_weight[0]), gather_dp(jnp.concatenate(own_kv, 1))]
        gain_total = jnp.zeros((1, width), F32)
        hidden = first_in
        for tick in range(TICKS):
            if tick:
                hidden = jnp.where(first == 1, balanced[1], shifted(outgoing, "section", 1))
                grad_in = jnp.where(
                    last == 1, loss_grad[1, 0], shifted(going_back, "section", -1)
                )
                mixed_work = project_mix_work(gather(hidden))
                heads, _ = whole_scatter([grad_in], [out_parts])
            else:
                mixed_work = mix_work(states[2], new_docs[0])
            (mixed,) = call(mixed_work, [shape(length, query_cols, BF16)])
            (outgoing,) = call(out_work(hidden, gather(mixed)), sent_type[:1])
            query_grad, kv_grad, aside = call(
                Work(
                    functools.partial(heads_body, kv_heads, len(heads)),
                    [states[tick], old_docs[tick], *heads],
                ),
                [
                    shape(length, query_cols, BF16),
                    shape(length, 2 * head_cols, F32 if bit_count else BF16),
                    shape(length, HEAD_SIZE, BF16),
                ],
            )
            grads = [jnp.concatenate([query_grad, kv_grad.astype(BF16)], 1)]
            if bit_count:
                kv_grad = jnp.stack([kv_grad[:, :head_cols], kv_grad[:, head_cols:]])
                for bit in reversed(range(bit_count)):
                    half = kv_grad.shape[-1] // 2
                    low_side = tensor_pos >> bit & 1 == 0
                    keep = jnp.where(low_side, kv_grad[..., :half], kv_grad[..., half:])
                    outward = jnp.where(low_side, kv_grad[..., half:], kv_grad[..., :half])
                    kv_grad = keep + exchange(outward.astype(BF16), "tensor", 1 << bit).astype(F32)
                grads = [query_grad, jnp.concatenate([kv_grad[0], kv_grad[1]], 1).astype(BF16)]
            terms, sides = whole_scatter(grads, grad_groups, aside)
            going_back, gain_term = call(result_work(tick, grad_in, terms, sides), sent_type)
            gain_total = gain_total + gain_term
    gain_total = gain_total + sum(exchange(gain_total, "dp", mask) for mask in (3, 2, 1))
    gain_grad = gain_total / math.sqrt(TICKS * replicas * length)
    return (outgoing[None, None], going_back[None, None], gain_grad)


def solution(mesh):
    return jax.shard_map(
        local,
        mesh=mesh,
        in_specs=(
            P("section", "dp", None, "tensor"),
            P(None, "dp", None, "tensor"),
            P(None, "section", "dp", None, "tensor"),
            P("section", "dp", None, "tensor"),
            P(None, "dp", None, "tensor"),
            P("section", "tensor"),
            P("section", "dp", "tensor"),
            P("section", "dp", "tensor"),
            P("section", "dp", "tensor"),
            P("section", "dp", "tensor"),
            P(),
            P(),
            P(None, "dp", None),
            P(None, "section", "dp", None),
        ),
        out_specs=(
            P("section", "dp", None, "tensor"),
            P("section", "dp", None, "tensor"),
            P("section", "tensor"),
        ),
        check_vma=False,
    )
```
